512 devices in a mesh: heads: 8 (over z_lo, core), tm: 64 (over x, y, z_hi).
Axes of the slice: x: 4, y: 8, z: 8 (z_hi: 2, z_lo: 4; z = z_hi * 4 + z_lo), core: 2. Of those that a mesh axis runs over, the one named last changes fastest.
Arguments:
- queries: bfloat16 [16384, 3072], P('tm', 'heads'), parts along dimension 1, may hold values from -8 to 8
- keys: bfloat16 [16384, 3072], P('tm', 'heads'), parts along dimension 1, may hold values from -8 to 8
- values: bfloat16 [16384, 3072], P('tm', 'heads'), parts along dimension 1, may hold values from -6 to 6
- positions: int32 [3, 16384], P(None, 'tm'), may hold values from 0 to 79, as said below
- tile_masks: int32 [128, 8, 2], P('tm'), may hold values from 0 to 1, as said below
- sink_index: int32 [256], replicated, may hold values from 0 to 3599, as said below
Outputs:
- attended: bfloat16 [16384, 3072], P('tm', 'heads'), parts along dimension 1
The draws below stay inside these ranges and needn't reach their ends.
There are 8 independent parts, one for each index of `heads`. The reference program is written for one: setup_inputs(seed, part) draws one part's arguments, and reference() takes and returns one part's arrays. A program takes and returns all parts, laid end to end along the dimension named above; an argument that names none is the same for every part. Nothing has to cross between parts.
Inputs may be any that keep to these rules, and one draw needn't show every extreme that they name: `positions`: consecutive tokens of the latent video of 33 x 45 x 80, row by row, from some starting token. `tile_masks`: tiles of farther partners are kept less often. `sink_index`: distinct rows among the first min(16384, 3600) of the window.
All inputs are finite; a program needn't handle non-finite values.
Results may differ from the reference program's by a relative error of at most 0.0085.
The reference program's roundings to bfloat16 on the way count: a program that leaves them out, or rounds other values in their place, can miss the bound.
Values may be sent and summed in bfloat16 or wider, within the bound.
A program may use at most 64 MiB of HBM per device.

```python
import jax
import jax.numpy as jnp
from jax import lax

HG = 3
HD = 128
TILE = 128
NOFF = 4
SINK = 256
LAT_T = 33
LAT_H = 45
LAT_W = 80
TOK_DEV = 256
TOKENS = 16384
N_TM = 64


def paired_draw(key):
    base = jax.random.fold_in(key, 7)
    first_key, second_key = jax.random.split(base, 2)
    feature_width = HG * HD
    query_data = jnp.clip(jax.random.normal(first_key, (TOKENS, feature_width)), -6.0, 6.0)
    key_data = jnp.clip(jax.random.normal(second_key, (TOKENS, feature_width)), -6.0, 6.0)
    return (query_data.astype(jnp.float32), key_data.astype(jnp.float32))


def draw_queries(key, part):
    return paired_draw(key)[0].astype(jnp.bfloat16)


def draw_keys(key, part):
    return paired_draw(key)[1].astype(jnp.bfloat16)


def draw_positions(key, part):
    frame_size = LAT_H * LAT_W
    start_token = jax.random.randint(jax.random.fold_in(key, 3), (), 0, LAT_T * frame_size - TOKENS + 1)
    global_ids = start_token + jnp.arange(TOKENS, dtype=jnp.int32)
    frame_ids = global_ids // frame_size
    row_ids = global_ids // LAT_W % LAT_H
    column_ids = global_ids % LAT_W
    return jnp.stack([frame_ids, row_ids, column_ids], axis=0).astype(jnp.int32)


def draw_tile_masks(key, part):
    tile_draw = jax.random.randint(jax.random.fold_in(key, 5), (TOKENS // TILE, 2 * NOFF, TOK_DEV // TILE), 0, NOFF + 1)
    distance = (jnp.arange(2 * NOFF, dtype=jnp.int32) % NOFF + 1)[None, :, None]
    return (tile_draw < NOFF + 1 - distance).astype(jnp.int32)


def draw_sink_index(key, part):
    first_rows = min(TOKENS, LAT_H * LAT_W)
    shuffled = jax.random.permutation(jax.random.fold_in(key, 9), first_rows - 2) + 1
    middle = shuffled[:SINK - 2].astype(jnp.int32)
    return jnp.concatenate([jnp.zeros((1,), jnp.int32), middle, jnp.full((1,), first_rows - 1, jnp.int32)]).astype(jnp.int32)


def block_levels(stream_key, shape, cuts, least, largest):
    level, own = 1.0, jax.random.fold_in(stream_key, 6)
    for dim, shards_of in cuts:
        draws = jnp.exp(jax.random.uniform(jax.random.fold_in(own, dim), (shards_of,), jnp.float32, least / len(cuts), largest / len(cuts)))
        level = level * jnp.repeat(draws, shape[dim] // shards_of).reshape([-1 if axis == dim else 1 for axis in range(len(shape))])
    return level


def noise(stream_key, dims, spread, limit, cuts=(), held_as=jnp.bfloat16):
    drawn = jax.random.normal(stream_key, dims, jnp.float32) * spread
    if len(cuts) > 0:
        drawn = block_levels(stream_key, dims, cuts, -0.22, 0.18) * drawn
    return jnp.clip(drawn, min=-limit, max=limit).astype(held_as)


def setup_inputs(seed: int = 0, part: int = 0) -> dict:
    key_of = jax.random.split(jax.random.key(seed), 7)
    part_keys = jax.random.split(jax.random.fold_in(key_of[6], part), 7)
    queries = draw_queries(jax.random.fold_in(jax.random.fold_in(key_of[6], part), 71), part)
    keys = draw_keys(jax.random.fold_in(jax.random.fold_in(key_of[6], part), 71), part)
    values = noise(part_keys[2], (TOKENS, HG * HD), 1.0, 6.0, ((0, 64),))
    positions = draw_positions(jax.random.fold_in(key_of[6], 71), part)
    tile_masks = draw_tile_masks(jax.random.fold_in(key_of[6], 71), part)
    sink_index = draw_sink_index(jax.random.fold_in(key_of[6], 71), part)
    return {"queries": queries, "keys": keys, "values": values, "positions": positions, "tile_masks": tile_masks, "sink_index": sink_index}


def rotate(row_data, position, factor):
    row_count = row_data.shape[0]
    first_size = HD // 8
    second_size = (HD - HD // 8) // 2
    section_sizes = (first_size, second_size, HD - first_size - second_size)
    angle_list = []
    for axis_id in range(3):
        section_width = section_sizes[axis_id]
        inverse = 256.0 ** (-jnp.arange(0, section_width, 2).astype(jnp.float32) / section_width)
        angle_list.append(position[axis_id].astype(jnp.float32)[:, None] * inverse[None, :])
    angle_all = jnp.concatenate(angle_list, axis=1)
    cosine = jnp.cos(angle_all)[:, None, :]
    sine_part = jnp.sin(angle_all)[:, None, :]
    pair_view = row_data.astype(jnp.float32).reshape(row_count, HG, HD // 2, 2)
    even_part = pair_view[..., 0]
    odd_part = pair_view[..., 1]
    turned = jnp.stack([even_part * cosine - odd_part * sine_part, even_part * sine_part + odd_part * cosine], axis=-1)
    return (turned * factor).reshape(row_count, HG * HD)


def reference(queries, keys, values, positions, tile_masks, sink_index):
    q_rot = rotate(queries, positions, HD ** -0.5).astype(jnp.bfloat16)
    k_rot = rotate(keys, positions, 1.0).astype(jnp.bfloat16)
    sink_keys = k_rot[sink_index].reshape(SINK, HG, HD)
    sink_values = values[sink_index].reshape(SINK, HG, HD)
    shards = N_TM
    tiles = TOK_DEV // TILE
    query_blocks = q_rot.reshape(shards, TOK_DEV, HG, HD)
    key_blocks = k_rot.reshape(shards, TOK_DEV, HG, HD)
    value_blocks = values.reshape(shards, TOK_DEV, HG, HD)
    mask_blocks = tile_masks.reshape(shards, tiles, 2 * NOFF, tiles)
    offset_list = [0] + list(range(1, NOFF + 1)) + [-step for step in range(1, NOFF + 1)]

    def one_shard(shard_id):
        key_list = []
        value_list = []
        mask_list = []
        for offset in offset_list:
            other = shard_id + offset
            inside = ((other >= 0) & (other < shards)).astype(jnp.float32)
            clipped = jnp.clip(other, 0, shards - 1).astype(jnp.int32)
            key_list.append(key_blocks[clipped])
            value_list.append(value_blocks[clipped])
            if offset == 0:
                tile_keep = jnp.ones((tiles, tiles), jnp.float32)
            elif offset > 0:
                tile_keep = mask_blocks[shard_id][:, offset - 1, :].astype(jnp.float32)
            else:
                tile_keep = mask_blocks[shard_id][:, NOFF - offset - 1, :].astype(jnp.float32)
            mask_list.append(tile_keep * inside)
        key_all = jnp.concatenate(key_list + [sink_keys], axis=0).astype(jnp.float32)
        value_all = jnp.concatenate(value_list + [sink_values], axis=0).astype(jnp.float32)
        keep_tiles = jnp.concatenate(mask_list, axis=1)
        keep_rows = jnp.repeat(jnp.repeat(keep_tiles, TILE, axis=0), TILE, axis=1)
        keep_mask = jnp.concatenate([keep_rows, jnp.ones((TOK_DEV, SINK), jnp.float32)], axis=1)[:, None, :]
        query_here = query_blocks[shard_id].astype(jnp.float32)
        scores = jnp.einsum('qhd,khd->qhk', query_here, key_all, precision=lax.Precision.HIGHEST)
        masked = jnp.where(keep_mask > 0, scores, -1e30)
        row_max = jnp.max(masked, axis=2)
        weights = jnp.exp(masked - row_max[:, :, None]) * keep_mask
        totals = jnp.sum(weights, axis=2)
        rounded = weights.astype(jnp.bfloat16)
        rounded = lax.optimization_barrier(rounded).astype(jnp.float32)
        weighted = jnp.einsum('qhk,khd->qhd', rounded, value_all, precision=lax.Precision.HIGHEST)
        return (weighted / totals[:, :, None]).astype(jnp.bfloat16)

    result = lax.map(one_shard, jnp.arange(shards, dtype=jnp.int32))
    return result.reshape(TOKENS, HG * HD)
```

```python
import functools

import jax
import jax.numpy as jnp
from jax import lax
from jax.experimental import pallas as pl
from jax.experimental.pallas import tpu as pltpu
from jax.sharding import PartitionSpec as P

MESH = pl.DeviceIdType.MESH
HG = 3
HD = 128
ROWS = 256
TILE = 128
SINK = 256
NX, NY = 4, 8
NP = NX * NY
CH = 16
MASKED = -1e30
FLOOR = -1e28
BF = jnp.bfloat16
F32 = jnp.float32
NT = (((1,), (1,)), ((), ()))


def iota(shape, dim):
    return lax.broadcasted_iota(jnp.int32, shape, dim)


def kernel(
    q_ref, k_ref, v_ref, pos_ref, sink_ref, mask_ref, out_ref,
    kv, qb, bias_own, bias_send, bias_recv, acc, ml, o_send, o_recv, ml_recv,
    ptab, tab, scat, sink_bias,
    s_kv, r_kv, s_q, r_q, s_b, r_b, s_sc, r_sc, s_y, r_y, s_x, r_x, s_o, r_o, s_ml, r_ml,
):
    head = lax.axis_index("heads")
    me = lax.axis_index("tm")
    z = me % 2
    p = me // 2
    x = p // NY
    y = p % NY
    kvi = x % 2
    half = x // 2

    def dev(pp, zz):
        return (head, pp * 2 + zz)

    def remote(src, dst, ssem, rsem, target):
        return pltpu.make_async_remote_copy(
            src_ref=src, dst_ref=dst, send_sem=ssem, recv_sem=rsem,
            device_id=target, device_id_type=MESH,
        )

    partner = dev(p, 1 - z)
    after = dev((p + 1) % NP, z)
    before = dev((p + NP - 1) % NP, z)

    barrier = pltpu.get_barrier_semaphore()
    pl.semaphore_signal(barrier, inc=1, device_id=partner, device_id_type=MESH)

    def greet(i, carry):
        pl.semaphore_signal(barrier, inc=1, device_id=dev((p + i) % NP, z), device_id_type=MESH)
        return carry

    lax.fori_loop(1, NP, greet, 0)

    d_of = iota((HD, ROWS), 0)
    first = d_of < 16
    second = d_of < 72
    posf = pos_ref[...].astype(F32)
    coord = jnp.where(first, posf[0:1], jnp.where(second, posf[1:2], posf[2:3]))
    pair = jnp.where(first, d_of, jnp.where(second, d_of - 16, d_of - 72)) // 2
    width = jnp.where(first, 16.0, 56.0).astype(F32)
    inverse = jnp.exp2(pair.astype(F32) * (-16.0) / width)
    angle = (coord * inverse).T
    lane = iota((ROWS, HD), 1)
    cosine = jnp.cos(angle)
    sine = jnp.sin(angle)
    sine = jnp.where(lane % 2 == 0, -sine, sine)
    r_id = iota((HD, HD), 0)
    c_id = iota((HD, HD), 1)
    swap = (r_id + 1 - 2 * (r_id % 2) == c_id).astype(BF)
    eye = (r_id == c_id).astype(BF)

    def rotated(ref, h, factor):
        part = ref[:, h * HD:(h + 1) * HD]
        other = jnp.dot(part, swap, preferred_element_type=F32)
        return ((part.astype(F32) * cosine + other * sine) * factor).astype(BF)

    for h in range(HG):
        kv[2, h, 0:ROWS, :] = rotated(k_ref, h, 1.0)
        turned = lax.dot_general(
            eye, v_ref[:, h * HD:(h + 1) * HD], NT, preferred_element_type=F32
        ).astype(BF)
        kv[2, h, ROWS:ROWS + HD, :] = turned[:, 0:TILE]
        kv[2, h, ROWS + HD:ROWS + 2 * HD, :] = turned[:, TILE:]
    for h in range(HG):
        qb[0, h] = rotated(q_ref, h, HD ** -0.5)

    sink_col = jnp.broadcast_to(sink_ref[...].astype(F32), (HD, SINK)).T.astype(jnp.int32)
    sink_bias[...] = jnp.where((sink_col // ROWS) % 2 == z, 0.0, MASKED).astype(F32)

    @pl.when(x == 0)
    def _():
        local = sink_col - me * ROWS
        hot = jnp.concatenate([local == lane, local == lane + HD], axis=1).astype(F32).astype(BF)
        for h in range(HG):
            cols = slice(h * HD, (h + 1) * HD)
            ptab[0, :, cols] = jnp.dot(
                hot, kv[2, h, 0:ROWS, :], preferred_element_type=F32
            ).astype(BF)
            ptab[1, :, cols] = jnp.dot(
                hot, v_ref[:, cols], preferred_element_type=F32
            ).astype(BF)

    wide = iota((1, ROWS), 1) < TILE

    def mask_row(offset, kt):
        slot = offset - 1 if offset > 0 else 4 - offset - 1
        other = me + offset
        inside = jnp.where((other >= 0) & (other < 2 * NP), 1, 0)
        both = [
            ((mask_ref[qt, slot, kt] * inside).astype(F32) - 1.0) * (-MASKED) for qt in range(2)
        ]
        return jnp.where(wide, both[0], both[1])

    for i, offset in enumerate((-4, -2, 2, 4)):
        for kt in range(2):
            bias_own[2 * i + kt:2 * i + kt + 1, :] = mask_row(offset, kt)
    for i, offset in enumerate((-3, -1, 1, 3)):
        for kt in range(2):
            bias_send[2 * i + kt:2 * i + kt + 1, :] = mask_row(offset, kt)

    pl.semaphore_wait(barrier, NP)

    def scatter(i):
        t = (p + i) % NP
        tx = t // NY
        row = pl.multiple_of((tx // 2) * (SINK // 2) + (t % NY) * CH, CH)
        return remote(
            ptab.at[tx % 2, pl.ds(row, CH)], scat.at[y], s_sc.at[i], r_sc.at[y], dev(t, z)
        )

    @pl.when(x == 0)
    def _():
        def go(i, carry):
            scatter(i).start()
            return carry

        lax.fori_loop(1, NP, go, 0)
        scat[y] = ptab[0, pl.ds(pl.multiple_of(y * CH, CH), CH), :]

    bias_copy = remote(bias_send, bias_recv, s_b, r_b, partner)
    bias_copy.start()
    q_copies = [remote(qb.at[0, h], qb.at[1, h], s_q.at[h], r_q.at[h], partner) for h in range(HG)]
    up = [remote(kv.at[2, h], kv.at[1, h], s_kv.at[0, h], r_kv.at[0, h], after) for h in range(HG)]
    down = [
        remote(kv.at[2, h], kv.at[3, h], s_kv.at[1, h], r_kv.at[1, h], before) for h in range(HG)
    ]
    up2 = [remote(kv.at[1, h], kv.at[0, h], s_kv.at[2, h], r_kv.at[2, h], after) for h in range(HG)]
    down2 = [
        remote(kv.at[3, h], kv.at[4, h], s_kv.at[3, h], r_kv.at[3, h], before) for h in range(HG)
    ]
    for h in range(HG):
        up[h].start()
        down[h].start()
        q_copies[h].start()

    for t in range(2):
        for h in range(HG):
            ml[t, h, 0:1, :] = jnp.full((1, ROWS), FLOOR, F32)
            ml[t, h, 1:2, :] = jnp.zeros((1, ROWS), F32)
            acc[t, h] = jnp.zeros((HD, ROWS), F32)

    def attend(t, h, blocks):
        query = qb[t, h]
        m_old = ml[t, h, 0:1, :]
        m_new = m_old
        scores = []
        for key, _, rows, key_bias in blocks:
            s = lax.dot_general(key(), query, NT, preferred_element_type=F32)
            if key_bias is not None:
                s = s + key_bias()
            for kt in range(2):
                part = jnp.max(s[kt * TILE:(kt + 1) * TILE], axis=0, keepdims=True)
                m_new = jnp.maximum(m_new, part if rows is None else part + rows[kt])
            scores.append(s)
        alpha = jnp.exp(m_old - m_new)
        total = ml[t, h, 1:2, :] * alpha
        result = acc[t, h] * alpha
        for (_, value, rows, _), s in zip(blocks, scores):
            weights = []
            for kt in range(2):
                level = m_new if rows is None else m_new - rows[kt]
                w = jnp.exp(s[kt * TILE:(kt + 1) * TILE] - level)
                total = total + jnp.sum(w, axis=0, keepdims=True)
                weights.append(w.astype(BF))
            result = result + jnp.dot(
                value(), jnp.concatenate(weights, axis=0), preferred_element_type=F32
            )
        acc[t, h] = result
        ml[t, h, 0:1, :] = m_new
        ml[t, h, 1:2, :] = total

    def shard_block(slot, h, rows):
        def key():
            return kv[slot, h, 0:ROWS, :]

        def value():
            return jnp.concatenate(
                [kv[slot, h, ROWS:ROWS + HD, :], kv[slot, h, ROWS + HD:ROWS + 2 * HD, :]], axis=1
            )

        return (key, value, rows, None)

    def own_rows(i):
        return [bias_own[2 * i + kt:2 * i + kt + 1, :] for kt in range(2)]

    def their_rows(even, odd):
        return [
            jnp.where(
                z == 0,
                bias_recv[2 * even + kt:2 * even + kt + 1, :],
                bias_recv[2 * odd + kt:2 * odd + kt + 1, :],
            )
            for kt in range(2)
        ]

    def sink_block(h):
        cols = slice(h * HD, (h + 1) * HD)

        def value():
            return lax.dot_general(eye, tab[1, :, cols], NT, preferred_element_type=F32).astype(BF)

        def key_bias():
            b = sink_bias[...]
            return jnp.concatenate([b, b], axis=1)

        return (lambda: tab[0, :, cols], value, None, key_bias)

    attend(0, 0, [shard_block(2, 0, None)])

    def arrived(i):
        return remote(
            ptab.at[0, pl.ds(0, CH)], scat.at[i], s_sc.at[0], r_sc.at[i], partner
        )

    def take(i, carry):
        @pl.when((x > 0) | (y != i))
        def _():
            arrived(i).wait_recv()

        return carry

    lax.fori_loop(0, NY, take, 0)
    chunk = scat[0].astype(F32)
    for i in range(1, NY):
        chunk = chunk + scat[i].astype(F32)
    base = half * (SINK // 2)

    def chunk_at(yy):
        return tab.at[kvi, pl.ds(pl.multiple_of(base + yy * CH, CH), CH)]

    tab[kvi, pl.ds(pl.multiple_of(base + y * CH, CH), CH), :] = chunk.astype(BF)

    def along_y(i):
        return remote(
            chunk_at(y), chunk_at(y), s_y.at[i], r_y.at[i], dev(x * NY + (y + i) % NY, z)
        )

    def from_y(i):
        there = chunk_at((y + NY - i) % NY)
        return remote(there, there, s_y.at[i], r_y.at[i], partner)

    def send_y(i, carry):
        along_y(i).start()
        return carry

    lax.fori_loop(1, NY, send_y, 0)

    for h in range(HG):
        up[h].wait_recv()
        up2[h].start()
        down[h].wait_recv()
        down2[h].start()
        if h == 0:
            attend(0, 1, [shard_block(2, 1, None)])
        if h == 1:
            attend(0, 2, [shard_block(2, 2, None)])

            def take_y(i, carry):
                from_y(i).wait_recv()
                return carry

            lax.fori_loop(1, NY, take_y, 0)

            def quarter(xx):
                row = pl.multiple_of((xx // 2) * (SINK // 2), SINK // 2)
                return tab.at[xx % 2, pl.ds(row, SINK // 2)]

            def along_x(i):
                return remote(
                    quarter(x), quarter(x), s_x.at[i], r_x.at[i], dev(((x + i) % NX) * NY + y, z)
                )

            def from_x(i):
                there = quarter((x + NX - i) % NX)
                return remote(there, there, s_x.at[i], r_x.at[i], partner)

            for i in range(1, NX):
                along_x(i).start()

    bias_copy.wait_recv()
    for h in range(HG):
        q_copies[h].wait_recv()
        attend(0, h, [shard_block(1, h, own_rows(1)), shard_block(3, h, own_rows(2))])
        attend(
            1,
            h,
            [
                shard_block(1, h, their_rows(0, 1)),
                shard_block(2, h, their_rows(1, 2)),
                shard_block(3, h, their_rows(2, 3)),
            ],
        )
    for i in range(1, NX):
        from_x(i).wait_recv()
    for h in range(HG):
        attend(1, h, [sink_block(h)])
        attend(0, h, [sink_block(h)])

    far = 4 * (1 - z)
    o_copies = []
    for h in range(HG):
        up2[h].wait_recv()
        down2[h].wait_recv()
        attend(1, h, [shard_block(far, h, their_rows(3, 0))])
        o_send[h] = acc[1, h].astype(BF)
        o_copies.append(remote(o_send.at[h], o_recv.at[h], s_o.at[h], r_o.at[h], partner))
        o_copies[-1].start()
        o_copies.append(remote(ml.at[1, h], ml_recv.at[h], s_ml.at[h], r_ml.at[h], partner))
        o_copies[-1].start()
        attend(0, h, [shard_block(0, h, own_rows(0)), shard_block(4, h, own_rows(3))])

    r_big = iota((ROWS, ROWS), 0)
    c_big = iota((ROWS, ROWS), 1)
    eye_big = (r_big == c_big).astype(BF)
    for h in range(HG):
        o_copies[2 * h].wait_recv()
        o_copies[2 * h + 1].wait_recv()
        m_a = ml[0, h, 0:1, :]
        m_b = ml_recv[h, 0:1, :]
        m_all = jnp.maximum(m_a, m_b)
        scale_a = jnp.exp(m_a - m_all)
        scale_b = jnp.exp(m_b - m_all)
        total = ml[0, h, 1:2, :] * scale_a + ml_recv[h, 1:2, :] * scale_b
        result = acc[0, h] * scale_a + o_recv[h].astype(F32) * scale_b
        result = (result / total).astype(BF)
        out_ref[:, h * HD:(h + 1) * HD] = lax.dot_general(
            eye_big, result, NT, preferred_element_type=F32
        ).astype(BF)

    @pl.when(x == 0)
    def _():
        def gone(i, carry):
            scatter(i).wait_send()
            return carry

        lax.fori_loop(1, NP, gone, 0)

    bias_copy.wait_send()
    for h in range(HG):
        for c in (q_copies, up, down, up2, down2):
            c[h].wait_send()

    def gone_y(i, carry):
        along_y(i).wait_send()
        return carry

    lax.fori_loop(1, NY, gone_y, 0)
    for i in range(1, NX):
        along_x(i).wait_send()
    for c in o_copies:
        c.wait_send()


def on_device(queries, keys, values, positions, tile_masks, sink_index):
    vmem = pl.BlockSpec(memory_space=pltpu.VMEM)
    smem = pl.BlockSpec(memory_space=pltpu.SMEM)
    dma = pltpu.SemaphoreType.DMA
    return pl.pallas_call(
        kernel,
        out_shape=jax.ShapeDtypeStruct(queries.shape, BF),
        in_specs=[vmem, vmem, vmem, vmem, vmem, smem],
        out_specs=vmem,
        scratch_shapes=[
            pltpu.VMEM((5, HG, 2 * ROWS, HD), BF),
            pltpu.VMEM((2, HG, ROWS, HD), BF),
            pltpu.VMEM((8, ROWS), F32),
            pltpu.VMEM((8, ROWS), F32),
            pltpu.VMEM((8, ROWS), F32),
            pltpu.VMEM((2, HG, HD, ROWS), F32),
            pltpu.VMEM((2, HG, 8, ROWS), F32),
            pltpu.VMEM((HG, HD, ROWS), BF),
            pltpu.VMEM((HG, HD, ROWS), BF),
            pltpu.VMEM((HG, 8, ROWS), F32),
            pltpu.VMEM((2, SINK, HG * HD), BF),
            pltpu.VMEM((2, SINK, HG * HD), BF),
            pltpu.VMEM((NY, CH, HG * HD), BF),
            pltpu.VMEM((SINK, HD), F32),
            dma((4, HG)), dma((4, HG)), dma((HG,)), dma((HG,)), dma, dma,
            dma((NP,)), dma((NY,)), dma((NY,)), dma((NY,)), dma((NX,)), dma((NX,)),
            dma((HG,)), dma((HG,)), dma((HG,)), dma((HG,)),
        ],
        compiler_params=pltpu.CompilerParams(
            collective_id=0, has_side_effects=True, vmem_limit_bytes=40 << 20
        ),
        cost_estimate=pl.CostEstimate(
            flops=2 * 11 * 2 * ROWS * ROWS * HD * HG, bytes_accessed=4 << 20,
            transcendentals=11 * ROWS * ROWS * HG,
        ),
    )(queries, keys, values, positions, sink_index[None, :], tile_masks)


def solution(mesh):
    in_specs = (
        P("tm", "heads"), P("tm", "heads"), P("tm", "heads"), P(None, "tm"), P("tm", None, None), P(),
    )
    return jax.shard_map(
        on_device, mesh=mesh, in_specs=in_specs, out_specs=P("tm", "heads"), check_vma=False
    )
```

```python
import functools

import jax
import jax.numpy as jnp
from jax import lax
from jax.experimental import pallas as pl
from jax.experimental.pallas import tpu as pltpu
from jax.sharding import PartitionSpec as P

MESH = pl.DeviceIdType.MESH
HG = 3
HD = 128
ROWS = 256
TILE = 128
SINK = 256
NX, NY = 4, 8
NP = NX * NY
CH = 16
KEPT = (0, 2)
MASKED = -1e30
FLOOR = -1e28
BF = jnp.bfloat16
F32 = jnp.float32
NT = (((1,), (1,)), ((), ()))


def iota(shape, dim):
    return lax.broadcasted_iota(jnp.int32, shape, dim)


def kernel(
    q_hbm, k_hbm, v_hbm, pos_hbm, sink_hbm, mask_hbm, out_ref,
    q_ref, k_ref, v_ref, pos_ref, sink_ref, mask_ref,
    kv, qb, bias_own, bias_send, bias_recv, acc, ml, o_send, o_recv, ml_recv,
    ptab, tab, quart, scat, z_send, z_recv, c_send,
    s_in, s_kv, r_kv, s_q, r_q, s_b, r_b, s_sc, r_sc, s_a, r_a, s_z, r_z, s_c, r_c, s_y, r_y,
    s_x, r_x, s_o, r_o, s_ml, r_ml,
):
    head = lax.axis_index("heads")
    me = lax.axis_index("tm")
    z = me % 2
    p = me // 2
    x = p // NY
    y = p % NY
    kvi = x % 2
    half = x // 2

    def dev(pp, zz):
        return (head, pp * 2 + zz)

    def remote(src, dst, ssem, rsem, target):
        return pltpu.make_async_remote_copy(
            src_ref=src, dst_ref=dst, send_sem=ssem, recv_sem=rsem,
            device_id=target, device_id_type=MESH,
        )

    partner = dev(p, 1 - z)
    after = dev((p + 1) % NP, z)
    before = dev((p + NP - 1) % NP, z)

    def on_y(i):
        return dev(x * NY + (y + i) % NY, z)

    def on_x(i):
        return dev(((x + i) % NX) * NY + y, z)

    near = [partner, after, before]
    near += [on_x(i) for i in range(1, NX)] + [on_y(i) for i in range(1, NY)]
    barrier = pltpu.get_barrier_semaphore()
    for target in near:
        pl.semaphore_signal(barrier, inc=1, device_id=target, device_id_type=MESH)

    loads = [
        pltpu.make_async_copy(src, dst, s_in.at[i])
        for i, (src, dst) in enumerate(
            [(pos_hbm, pos_ref), (k_hbm, k_ref), (v_hbm, v_ref), (sink_hbm, sink_ref),
             (mask_hbm, mask_ref), (q_hbm, q_ref)]
        )
    ]
    for c in loads:
        c.start()
    loads[0].wait()

    d_of = iota((HD, ROWS), 0)
    first = d_of < 16
    second = d_of < 72
    posf = pos_ref[...].astype(F32)
    coord = jnp.where(first, posf[0:1], jnp.where(second, posf[1:2], posf[2:3]))
    pair = jnp.where(first, d_of, jnp.where(second, d_of - 16, d_of - 72)) // 2
    width = jnp.where(first, 16.0, 56.0).astype(F32)
    inverse = jnp.exp2(pair.astype(F32) * (-16.0) / width)
    angle = (coord * inverse).T
    lane = iota((ROWS, HD), 1)
    cosine = jnp.cos(angle)
    sine = jnp.sin(angle)
    sine = jnp.where(lane % 2 == 0, -sine, sine)
    r_id = iota((HD, HD), 0)
    c_id = iota((HD, HD), 1)
    swap = (r_id + 1 - 2 * (r_id % 2) == c_id).astype(BF)
    eye = (r_id == c_id).astype(BF)

    def rotated(ref, h, factor):
        part = ref[:, h * HD:(h + 1) * HD]
        other = jnp.dot(part, swap, preferred_element_type=F32)
        return ((part.astype(F32) * cosine + other * sine) * factor).astype(BF)

    loads[1].wait()
    loads[2].wait()
    for h in range(HG):
        kv[2, h, 0:ROWS, :] = rotated(k_ref, h, 1.0)
        turned = lax.dot_general(
            eye, v_ref[:, h * HD:(h + 1) * HD], NT, preferred_element_type=F32
        ).astype(BF)
        kv[2, h, ROWS:ROWS + HD, :] = turned[:, 0:TILE]
        kv[2, h, ROWS + HD:ROWS + 2 * HD, :] = turned[:, TILE:]

    loads[3].wait()

    spread_to = [i for i in range(1, NX) if i not in KEPT]
    gets_quarter = functools.reduce(lambda a, b: a | b, [x == i for i in spread_to], x < 0)
    gets_chunk = functools.reduce(lambda a, b: a | b, [x == i for i in KEPT[1:]], x < 0)

    def spread(i):
        return remote(
            ptab.at[i % 2, pl.ds((i // 2) * (SINK // 2), SINK // 2)], quart,
            s_sc.at[i], r_sc, on_x(i),
        )

    @pl.when(x == 0)
    def _():
        sink_col = jnp.broadcast_to(sink_ref[...].astype(F32), (HD, SINK)).T.astype(jnp.int32)
        local = sink_col - me * ROWS
        hot = jnp.concatenate([local == lane, local == lane + HD], axis=1).astype(F32).astype(BF)
        for h in range(HG):
            cols = slice(h * HD, (h + 1) * HD)
            ptab[0, :, cols] = jnp.dot(
                hot, kv[2, h, 0:ROWS, :], preferred_element_type=F32
            ).astype(BF)
            ptab[1, :, cols] = jnp.dot(
                hot, v_ref[:, cols], preferred_element_type=F32
            ).astype(BF)

    pl.semaphore_wait(barrier, len(near))

    up = [remote(kv.at[2, h], kv.at[1, h], s_kv.at[0, h], r_kv.at[0, h], after) for h in range(HG)]
    down = [
        remote(kv.at[2, h], kv.at[3, h], s_kv.at[1, h], r_kv.at[1, h], before) for h in range(HG)
    ]
    up2 = [remote(kv.at[1, h], kv.at[0, h], s_kv.at[2, h], r_kv.at[2, h], after) for h in range(HG)]
    down2 = [
        remote(kv.at[3, h], kv.at[4, h], s_kv.at[3, h], r_kv.at[3, h], before) for h in range(HG)
    ]

    @pl.when(x == 0)
    def _():
        for i in spread_to:
            spread(i).start()

    def send_kv(h):
        up[h].start()
        down[h].start()

    send_kv(0)


    loads[4].wait()
    loads[5].wait()
    for h in range(HG):
        qb[0, h] = rotated(q_ref, h, HD ** -0.5)
    wide = iota((1, ROWS), 1) < TILE

    def mask_row(offset, kt):
        slot = offset - 1 if offset > 0 else 4 - offset - 1
        other = me + offset
        inside = jnp.where((other >= 0) & (other < 2 * NP), 1, 0)
        both = [
            ((mask_ref[qt, kt, slot] * inside).astype(F32) - 1.0) * (-MASKED) for qt in range(2)
        ]
        return jnp.where(wide, both[0], both[1])

    for i, offset in enumerate((-3, -1, 1, 3)):
        for kt in range(2):
            bias_send[2 * i + kt:2 * i + kt + 1, :] = mask_row(offset, kt)
    bias_copy = remote(bias_send, bias_recv, s_b, r_b, partner)
    bias_copy.start()
    q_copies = [remote(qb.at[0, h], qb.at[1, h], s_q.at[h], r_q.at[h], partner) for h in range(HG)]
    for h in range(HG):
        q_copies[h].start()
    for i, offset in enumerate((-4, -2, 2, 4)):
        for kt in range(2):
            bias_own[2 * i + kt:2 * i + kt + 1, :] = mask_row(offset, kt)


    for t in range(2):
        for h in range(HG):
            ml[t, h, 0:1, :] = jnp.full((1, ROWS), FLOOR, F32)
            ml[t, h, 1:2, :] = jnp.zeros((1, ROWS), F32)
            acc[t, h] = jnp.zeros((HD, ROWS), F32)

    def attend(t, h, blocks):
        query = qb[t, h]
        m_old = ml[t, h, 0:1, :]
        m_new = m_old
        scores = []
        for key, _, rows in blocks:
            s = lax.dot_general(key(), query, NT, preferred_element_type=F32)
            for kt in range(2):
                part = jnp.max(s[kt * TILE:(kt + 1) * TILE], axis=0, keepdims=True)
                m_new = jnp.maximum(m_new, part if rows is None else part + rows[kt])
            scores.append(s)
        alpha = jnp.exp(m_old - m_new)
        total = ml[t, h, 1:2, :] * alpha
        result = acc[t, h] * alpha
        for (_, value, rows), s in zip(blocks, scores):
            weights = []
            for kt in range(2):
                level = m_new if rows is None else m_new - rows[kt]
                w = jnp.exp(s[kt * TILE:(kt + 1) * TILE] - level)
                total = total + jnp.sum(w, axis=0, keepdims=True)
                weights.append(w.astype(BF))
            result = result + jnp.dot(
                value(), jnp.concatenate(weights, axis=0), preferred_element_type=F32
            )
        acc[t, h] = result
        ml[t, h, 0:1, :] = m_new
        ml[t, h, 1:2, :] = total

    def shard_block(slot, h, rows):
        def key():
            return kv[slot, h, 0:ROWS, :]

        def value():
            return jnp.concatenate(
                [kv[slot, h, ROWS:ROWS + HD, :], kv[slot, h, ROWS + HD:ROWS + 2 * HD, :]], axis=1
            )

        return (key, value, rows)

    def own_rows(i):
        return [bias_own[2 * i + kt:2 * i + kt + 1, :] for kt in range(2)]

    def their_rows(even, odd):
        return [
            jnp.where(
                z == 0,
                bias_recv[2 * even + kt:2 * even + kt + 1, :],
                bias_recv[2 * odd + kt:2 * odd + kt + 1, :],
            )
            for kt in range(2)
        ]

    def sink_block(h):
        cols = slice(h * HD, (h + 1) * HD)

        def value():
            return lax.dot_general(eye, tab[1, :, cols], NT, preferred_element_type=F32).astype(BF)

        return (lambda: tab[0, :, cols], value, None)

    def hop(h):
        up[h].wait_recv()
        up2[h].start()
        down[h].wait_recv()
        down2[h].start()

    def near_blocks(h):
        q_copies[h].wait_recv()
        attend(
            1,
            h,
            [
                shard_block(1, h, their_rows(0, 1)),
                shard_block(2, h, their_rows(1, 2)),
                shard_block(3, h, their_rows(2, 3)),
            ],
        )
        attend(0, h, [shard_block(1, h, own_rows(1)), shard_block(3, h, own_rows(2))])

    far = 4 * (1 - z)
    o_copies = [remote(o_send.at[h], o_recv.at[h], s_o.at[h], r_o.at[h], partner) for h in range(HG)]
    ml_copies = [
        remote(ml.at[1, h], ml_recv.at[h], s_ml.at[h], r_ml.at[h], partner) for h in range(HG)
    ]

    def far_blocks(h):
        up2[h].wait_recv()
        down2[h].wait_recv()
        attend(1, h, [shard_block(far, h, their_rows(3, 0))])
        o_send[h] = acc[1, h].astype(BF)
        o_copies[h].start()
        ml_copies[h].start()
        attend(0, h, [shard_block(0, h, own_rows(0)), shard_block(4, h, own_rows(3))])

    base = half * (SINK // 2)

    def chunk_at(yy):
        return tab.at[kvi, pl.ds(pl.multiple_of(base + yy * CH, CH), CH)]

    def quarter(xx):
        row = pl.multiple_of((xx // 2) * (SINK // 2), SINK // 2)
        return tab.at[xx % 2, pl.ds(row, SINK // 2)]

    def part_of(yy):
        return pl.ds(pl.multiple_of(yy * CH, CH), CH)

    def row_of(u, yy):
        return pl.ds(pl.multiple_of((u // 2) * (SINK // 2) + yy * CH, CH), CH)

    kept_copies = [
        remote(
            ptab.at[u % 2, row_of(u, (y + i) % NY)], scat.at[j, i], s_a.at[j, i], r_a.at[j, i], on_y(i)
        )
        for j, u in enumerate(KEPT) for i in range(1, NY)
    ]
    a_copies = [
        remote(quart.at[part_of((y + i) % NY)], scat.at[0, i], s_a.at[0, i], r_a.at[0, i], on_y(i))
        for i in range(1, NY)
    ]
    kept_z = remote(z_send, z_recv, s_z, r_z, partner)
    z_copy = remote(z_send.at[0], z_recv.at[0], s_z, r_z, partner)
    c_copies = [
        remote(c_send.at[j], tab.at[u % 2, row_of(u, y)], s_c.at[j], r_c, on_x(u))
        for j, u in enumerate(KEPT) if j > 0
    ]
    c_arrival = remote(c_send.at[0], chunk_at(y), s_c.at[0], r_c, partner)
    y_copies = [
        remote(chunk_at(y), chunk_at(y), s_y.at[i], r_y.at[i], on_y(i)) for i in range(1, NY)
    ]
    y_arrivals = [
        remote(chunk_at((y + NY - i) % NY), chunk_at((y + NY - i) % NY), s_y.at[i], r_y.at[i], partner)
        for i in range(1, NY)
    ]
    x_copies = [
        remote(quarter(x), quarter(x), s_x.at[i], r_x.at[i], on_x(i)) for i in range(1, NX)
    ]
    x_arrivals = [
        remote(quarter((x + NX - i) % NX), quarter((x + NX - i) % NX), s_x.at[i], r_x.at[i], partner)
        for i in range(1, NX)
    ]

    def sink_exchange():
        @pl.when(x == 0)
        def _():
            for c in kept_copies:
                c.start()

        @pl.when(gets_quarter)
        def _():
            spread(1).wait_recv()
            for c in a_copies:
                c.start()

    def sink_sum():
        @pl.when(x == 0)
        def _():
            for c in kept_copies:
                c.wait_recv()
            for j, u in enumerate(KEPT):
                chunk = ptab[u % 2, row_of(u, y), :].astype(F32)
                for i in range(1, NY):
                    chunk = chunk + scat[j, i].astype(F32)
                z_send[j] = chunk.astype(BF)
            kept_z.start()

        @pl.when(gets_quarter)
        def _():
            for c in a_copies:
                c.wait_recv()
            chunk = quart[part_of(y), :].astype(F32)
            for i in range(1, NY):
                chunk = chunk + scat[0, i].astype(F32)
            z_send[0] = chunk.astype(BF)
            z_copy.start()

    def sink_finish():
        @pl.when(x == 0)
        def _():
            kept_z.wait_recv()
            for j in range(1, len(KEPT)):
                c_send[j] = (z_send[j].astype(F32) + z_recv[j].astype(F32)).astype(BF)
                c_copies[j - 1].start()

        @pl.when(gets_quarter)
        def _():
            z_copy.wait_recv()

        @pl.when(gets_chunk)
        def _():
            c_arrival.wait_recv()

        @pl.when((x == 0) | gets_quarter)
        def _():
            chunk = z_send[0].astype(F32) + z_recv[0].astype(F32)
            tab[kvi, pl.ds(pl.multiple_of(base + y * CH, CH), CH), :] = chunk.astype(BF)

        for c in y_copies:
            c.start()

    def sink_along_x():
        for c in y_arrivals:
            c.wait_recv()
        for c in x_copies:
            c.start()

    attend(0, 0, [shard_block(2, 0, None)])
    send_kv(1)
    attend(0, 1, [shard_block(2, 1, None)])
    attend(0, 2, [shard_block(2, 2, None)])
    sink_exchange()
    hop(0)
    send_kv(2)
    bias_copy.wait_recv()
    near_blocks(0)
    sink_sum()
    hop(1)
    near_blocks(1)
    sink_finish()
    hop(2)
    far_blocks(0)
    near_blocks(2)
    sink_along_x()
    far_blocks(1)
    far_blocks(2)
    for c in x_arrivals:
        c.wait_recv()
    for h in range(HG):
        attend(0, h, [sink_block(h)])

    r_big = iota((ROWS, ROWS), 0)
    c_big = iota((ROWS, ROWS), 1)
    eye_big = (r_big == c_big).astype(BF)
    for h in range(HG):
        o_copies[h].wait_recv()
        ml_copies[h].wait_recv()
        m_a = ml[0, h, 0:1, :]
        m_b = ml_recv[h, 0:1, :]
        m_all = jnp.maximum(m_a, m_b)
        scale_a = jnp.exp(m_a - m_all)
        scale_b = jnp.exp(m_b - m_all)
        total = ml[0, h, 1:2, :] * scale_a + ml_recv[h, 1:2, :] * scale_b
        result = acc[0, h] * scale_a + o_recv[h].astype(F32) * scale_b
        result = (result / total).astype(BF)
        out_ref[:, h * HD:(h + 1) * HD] = lax.dot_general(
            eye_big, result, NT, preferred_element_type=F32
        ).astype(BF)

    @pl.when(x == 0)
    def _():
        for i in spread_to:
            spread(i).wait_send()

    for group in (q_copies, up, down, up2, down2, o_copies, ml_copies, y_copies, x_copies):
        for c in group:
            c.wait_send()
    bias_copy.wait_send()

    @pl.when(x == 0)
    def _():
        kept_z.wait_send()
        for c in kept_copies + c_copies:
            c.wait_send()

    @pl.when(gets_quarter)
    def _():
        z_copy.wait_send()
        for c in a_copies:
            c.wait_send()


def on_device(queries, keys, values, positions, tile_masks, sink_index):
    anywhere = pl.BlockSpec(memory_space=pl.ANY)
    dma = pltpu.SemaphoreType.DMA
    shard = (ROWS, HG * HD)
    return pl.pallas_call(
        kernel,
        out_shape=jax.ShapeDtypeStruct(shard, BF),
        in_specs=[anywhere] * 6,
        out_specs=pl.BlockSpec(memory_space=pltpu.VMEM),
        scratch_shapes=[
            pltpu.VMEM(shard, BF),
            pltpu.VMEM(shard, BF),
            pltpu.VMEM(shard, BF),
            pltpu.VMEM((3, ROWS), jnp.int32),
            pltpu.VMEM((1, SINK), jnp.int32),
            pltpu.SMEM((2, 2, 8), jnp.int32),
            pltpu.VMEM((5, HG, 2 * ROWS, HD), BF),
            pltpu.VMEM((2, HG, ROWS, HD), BF),
            pltpu.VMEM((8, ROWS), F32),
            pltpu.VMEM((8, ROWS), F32),
            pltpu.VMEM((8, ROWS), F32),
            pltpu.VMEM((2, HG, HD, ROWS), F32),
            pltpu.VMEM((2, HG, 8, ROWS), F32),
            pltpu.VMEM((HG, HD, ROWS), BF),
            pltpu.VMEM((HG, HD, ROWS), BF),
            pltpu.VMEM((HG, 8, ROWS), F32),
            pltpu.VMEM((2, SINK, HG * HD), BF),
            pltpu.VMEM((2, SINK, HG * HD), BF),
            pltpu.VMEM((SINK // 2, HG * HD), BF),
            pltpu.VMEM((len(KEPT), NY, CH, HG * HD), BF),
            pltpu.VMEM((len(KEPT), CH, HG * HD), BF),
            pltpu.VMEM((len(KEPT), CH, HG * HD), BF),
            pltpu.VMEM((len(KEPT), CH, HG * HD), BF),
            dma((6,)),
            dma((4, HG)), dma((4, HG)), dma((HG,)), dma((HG,)), dma, dma,
            dma((NX,)), dma, dma((len(KEPT), NY)), dma((len(KEPT), NY)), dma, dma,
            dma((len(KEPT),)), dma, dma((NY,)), dma((NY,)),
            dma((NX,)), dma((NX,)), dma((HG,)), dma((HG,)), dma((HG,)), dma((HG,)),
        ],
        compiler_params=pltpu.CompilerParams(
            collective_id=0, has_side_effects=True, vmem_limit_bytes=60 << 20
        ),
        cost_estimate=pl.CostEstimate(
            flops=2 * 10 * 2 * ROWS * ROWS * HD * HG, bytes_accessed=4 << 20,
            transcendentals=10 * ROWS * ROWS * HG,
        ),
    )(queries, keys, values, positions, sink_index[None, :], tile_masks.transpose(0, 2, 1))


def solution(mesh):
    in_specs = (
        P("tm", "heads"), P("tm", "heads"), P("tm", "heads"), P(None, "tm"), P("tm", None, None), P(),
    )
    return jax.shard_map(
        on_device, mesh=mesh, in_specs=in_specs, out_specs=P("tm", "heads"), check_vma=False
    )
```

```python
import functools

import jax
import jax.numpy as jnp
from jax import lax
from jax.experimental import pallas as pl
from jax.experimental.pallas import tpu as pltpu
from jax.sharding import PartitionSpec as P

MESH = pl.DeviceIdType.MESH
HG = 3
HD = 128
ROWS = 256
TILE = 128
SINK = 256
NX, NY = 4, 8
NP = NX * NY
CH = 16
KEPT = (0, 2)
MASKED = -1e30
FLOOR = -1e28
BF = jnp.bfloat16
F32 = jnp.float32
NT = (((1,), (1,)), ((), ()))


def iota(shape, dim):
    return lax.broadcasted_iota(jnp.int32, shape, dim)


def kernel(
    q_hbm, k_hbm, v_hbm, pos_hbm, sink_hbm, mask_hbm, out_ref,
    q_ref, k_ref, v_ref, pos_ref, sink_ref, mask_ref,
    kv, qb, bias_own, bias_send, bias_recv, acc, ml, o_send, o_recv, ml_recv,
    ptab, tab, quart, scat, z_send, z_recv, c_send,
    s_in, s_kv, r_kv, s_q, r_q, s_b, r_b, s_sc, r_sc, s_a, r_a, s_z, r_z, s_c, r_c, s_y, r_y,
    s_x, r_x, s_o, r_o, s_ml, r_ml,
):
    head = lax.axis_index("heads")
    me = lax.axis_index("tm")
    z = me % 2
    p = me // 2
    x = p // NY
    y = p % NY
    kvi = x % 2
    half = x // 2

    def dev(pp, zz):
        return (head, pp * 2 + zz)

    def remote(src, dst, ssem, rsem, target):
        return pltpu.make_async_remote_copy(
            src_ref=src, dst_ref=dst, send_sem=ssem, recv_sem=rsem,
            device_id=target, device_id_type=MESH,
        )

    partner = dev(p, 1 - z)
    after = dev((p + 1) % NP, z)
    before = dev((p + NP - 1) % NP, z)

    def on_y(i):
        return dev(x * NY + (y + i) % NY, z)

    def on_x(i):
        return dev(((x + i) % NX) * NY + y, z)

    near = [partner, after, before]
    near += [on_x(i) for i in range(1, NX)] + [on_y(i) for i in range(1, NY)]
    barrier = pltpu.get_barrier_semaphore()
    for target in near:
        pl.semaphore_signal(barrier, inc=1, device_id=target, device_id_type=MESH)

    loads = [
        pltpu.make_async_copy(src, dst, s_in.at[i])
        for i, (src, dst) in enumerate(
            [(pos_hbm, pos_ref), (k_hbm, k_ref), (v_hbm, v_ref), (sink_hbm, sink_ref),
             (mask_hbm, mask_ref), (q_hbm, q_ref)]
        )
    ]
    for c in loads:
        c.start()
    loads[0].wait()

    d_of = iota((HD, ROWS), 0)
    first = d_of < 16
    second = d_of < 72
    posf = pos_ref[...].astype(F32)
    coord = jnp.where(first, posf[0:1], jnp.where(second, posf[1:2], posf[2:3]))
    pair = jnp.where(first, d_of, jnp.where(second, d_of - 16, d_of - 72)) // 2
    width = jnp.where(first, 16.0, 56.0).astype(F32)
    inverse = jnp.exp2(pair.astype(F32) * (-16.0) / width)
    angle = (coord * inverse).T
    lane = iota((ROWS, HD), 1)
    cosine = jnp.cos(angle)
    sine = jnp.sin(angle)
    sine = jnp.where(lane % 2 == 0, -sine, sine)
    r_id = iota((HD, HD), 0)
    c_id = iota((HD, HD), 1)
    swap = (r_id + 1 - 2 * (r_id % 2) == c_id).astype(BF)
    eye = (r_id == c_id).astype(BF)

    def rotated(ref, h, factor):
        part = ref[:, h * HD:(h + 1) * HD]
        other = jnp.dot(part, swap, preferred_element_type=F32)
        return ((part.astype(F32) * cosine + other * sine) * factor).astype(BF)

    loads[1].wait()
    loads[2].wait()
    for h in range(HG):
        kv[2, h, 0:ROWS, :] = rotated(k_ref, h, 1.0)
        turned = lax.dot_general(
            eye, v_ref[:, h * HD:(h + 1) * HD], NT, preferred_element_type=F32
        ).astype(BF)
        kv[2, h, ROWS:ROWS + HD, :] = turned[:, 0:TILE]
        kv[2, h, ROWS + HD:ROWS + 2 * HD, :] = turned[:, TILE:]

    loads[3].wait()

    spread_to = [i for i in range(1, NX) if i not in KEPT]
    gets_quarter = functools.reduce(lambda a, b: a | b, [x == i for i in spread_to], x < 0)
    gets_chunk = functools.reduce(lambda a, b: a | b, [x == i for i in KEPT[1:]], x < 0)

    def spread(i):
        return remote(
            ptab.at[i % 2, pl.ds((i // 2) * (SINK // 2), SINK // 2)], quart,
            s_sc.at[i], r_sc, on_x(i),
        )

    @pl.when(x == 0)
    def _():
        sink_col = jnp.broadcast_to(sink_ref[...].astype(F32), (HD, SINK)).T.astype(jnp.int32)
        local = sink_col - me * ROWS
        hot = jnp.concatenate([local == lane, local == lane + HD], axis=1).astype(F32).astype(BF)
        for h in range(HG):
            cols = slice(h * HD, (h + 1) * HD)
            ptab[0, :, cols] = jnp.dot(
                hot, kv[2, h, 0:ROWS, :], preferred_element_type=F32
            ).astype(BF)
            ptab[1, :, cols] = jnp.dot(
                hot, v_ref[:, cols], preferred_element_type=F32
            ).astype(BF)

    pl.semaphore_wait(barrier, len(near))

    up = [remote(kv.at[2, h], kv.at[1, h], s_kv.at[0, h], r_kv.at[0, h], after) for h in range(HG)]
    down = [
        remote(kv.at[2, h], kv.at[3, h], s_kv.at[1, h], r_kv.at[1, h], before) for h in range(HG)
    ]
    up2 = [remote(kv.at[1, h], kv.at[0, h], s_kv.at[2, h], r_kv.at[2, h], after) for h in range(HG)]
    down2 = [
        remote(kv.at[3, h], kv.at[4, h], s_kv.at[3, h], r_kv.at[3, h], before) for h in range(HG)
    ]

    @pl.when(x == 0)
    def _():
        for i in spread_to:
            spread(i).start()

    def send_kv(h):
        up[h].start()
        down[h].start()

    def row_of(u, yy):
        return pl.ds(pl.multiple_of((u // 2) * (SINK // 2) + yy * CH, CH), CH)

    kept_copies = [
        remote(
            ptab.at[u % 2, row_of(u, (y + i) % NY)], scat.at[j, i], s_a.at[j, i], r_a.at[j, i], on_y(i)
        )
        for j, u in enumerate(KEPT) for i in range(1, NY)
    ]

    @pl.when(x == 0)
    def _():
        for c in kept_copies:
            c.start()

    send_kv(0)


    loads[4].wait()
    loads[5].wait()
    for h in range(HG):
        qb[0, h] = rotated(q_ref, h, HD ** -0.5)
    wide = iota((1, ROWS), 1) < TILE

    def mask_row(offset, kt):
        slot = offset - 1 if offset > 0 else 4 - offset - 1
        other = me + offset
        inside = jnp.where((other >= 0) & (other < 2 * NP), 1, 0)
        both = [
            ((mask_ref[qt, kt, slot] * inside).astype(F32) - 1.0) * (-MASKED) for qt in range(2)
        ]
        return jnp.where(wide, both[0], both[1])

    for i, offset in enumerate((-3, -1, 1, 3)):
        for kt in range(2):
            bias_send[2 * i + kt:2 * i + kt + 1, :] = mask_row(offset, kt)
    bias_copy = remote(bias_send, bias_recv, s_b, r_b, partner)
    bias_copy.start()
    q_copies = [remote(qb.at[0, h], qb.at[1, h], s_q.at[h], r_q.at[h], partner) for h in range(HG)]
    for h in range(HG):
        q_copies[h].start()
    for i, offset in enumerate((-4, -2, 2, 4)):
        for kt in range(2):
            bias_own[2 * i + kt:2 * i + kt + 1, :] = mask_row(offset, kt)


    for t in range(2):
        for h in range(HG):
            ml[t, h, 0:1, :] = jnp.full((1, ROWS), FLOOR, F32)
            ml[t, h, 1:2, :] = jnp.zeros((1, ROWS), F32)
            acc[t, h] = jnp.zeros((HD, ROWS), F32)

    def attend(t, h, blocks):
        query = qb[t, h]
        m_old = ml[t, h, 0:1, :]
        m_new = m_old
        scores = []
        for key, _, rows in blocks:
            s = lax.dot_general(key(), query, NT, preferred_element_type=F32)
            for kt in range(2):
                part = jnp.max(s[kt * TILE:(kt + 1) * TILE], axis=0, keepdims=True)
                m_new = jnp.maximum(m_new, part if rows is None else part + rows[kt])
            scores.append(s)
        alpha = jnp.exp(m_old - m_new)
        total = ml[t, h, 1:2, :] * alpha
        result = acc[t, h] * alpha
        for (_, value, rows), s in zip(blocks, scores):
            weights = []
            for kt in range(2):
                level = m_new if rows is None else m_new - rows[kt]
                w = jnp.exp(s[kt * TILE:(kt + 1) * TILE] - level)
                total = total + jnp.sum(w, axis=0, keepdims=True)
                weights.append(w.astype(BF))
            result = result + jnp.dot(
                value(), jnp.concatenate(weights, axis=0), preferred_element_type=F32
            )
        acc[t, h] = result
        ml[t, h, 0:1, :] = m_new
        ml[t, h, 1:2, :] = total

    def shard_block(slot, h, rows):
        def key():
            return kv[slot, h, 0:ROWS, :]

        def value():
            return jnp.concatenate(
                [kv[slot, h, ROWS:ROWS + HD, :], kv[slot, h, ROWS + HD:ROWS + 2 * HD, :]], axis=1
            )

        return (key, value, rows)

    def own_rows(i):
        return [bias_own[2 * i + kt:2 * i + kt + 1, :] for kt in range(2)]

    def their_rows(even, odd):
        return [
            jnp.where(
                z == 0,
                bias_recv[2 * even + kt:2 * even + kt + 1, :],
                bias_recv[2 * odd + kt:2 * odd + kt + 1, :],
            )
            for kt in range(2)
        ]

    def sink_block(h):
        cols = slice(h * HD, (h + 1) * HD)

        def value():
            return lax.dot_general(eye, tab[1, :, cols], NT, preferred_element_type=F32).astype(BF)

        return (lambda: tab[0, :, cols], value, None)

    def hop(h):
        up[h].wait_recv()
        up2[h].start()
        down[h].wait_recv()
        down2[h].start()

    def near_blocks(h):
        q_copies[h].wait_recv()
        attend(
            1,
            h,
            [
                shard_block(1, h, their_rows(0, 1)),
                shard_block(2, h, their_rows(1, 2)),
                shard_block(3, h, their_rows(2, 3)),
            ],
        )
        attend(0, h, [shard_block(1, h, own_rows(1)), shard_block(3, h, own_rows(2))])

    far = 4 * (1 - z)
    o_copies = [remote(o_send.at[h], o_recv.at[h], s_o.at[h], r_o.at[h], partner) for h in range(HG)]
    ml_copies = [
        remote(ml.at[1, h], ml_recv.at[h], s_ml.at[h], r_ml.at[h], partner) for h in range(HG)
    ]

    def far_blocks(h):
        up2[h].wait_recv()
        down2[h].wait_recv()
        attend(1, h, [shard_block(far, h, their_rows(3, 0))])
        o_send[h] = acc[1, h].astype(BF)
        o_copies[h].start()
        ml_copies[h].start()
        attend(0, h, [shard_block(0, h, own_rows(0)), shard_block(4, h, own_rows(3))])

    base = half * (SINK // 2)

    def chunk_at(yy):
        return tab.at[kvi, pl.ds(pl.multiple_of(base + yy * CH, CH), CH)]

    def quarter(xx):
        row = pl.multiple_of((xx // 2) * (SINK // 2), SINK // 2)
        return tab.at[xx % 2, pl.ds(row, SINK // 2)]

    def part_of(yy):
        return pl.ds(pl.multiple_of(yy * CH, CH), CH)

    a_copies = [
        remote(quart.at[part_of((y + i) % NY)], scat.at[0, i], s_a.at[0, i], r_a.at[0, i], on_y(i))
        for i in range(1, NY)
    ]
    kept_z = remote(z_send, z_recv, s_z, r_z, partner)
    z_copy = remote(z_send.at[0], z_recv.at[0], s_z, r_z, partner)
    c_copies = [
        remote(c_send.at[j], tab.at[u % 2, row_of(u, y)], s_c.at[j], r_c, on_x(u))
        for j, u in enumerate(KEPT) if j > 0
    ]
    c_arrival = remote(c_send.at[0], chunk_at(y), s_c.at[0], r_c, partner)
    y_copies = [
        remote(chunk_at(y), chunk_at(y), s_y.at[i], r_y.at[i], on_y(i)) for i in range(1, NY)
    ]
    y_arrivals = [
        remote(chunk_at((y + NY - i) % NY), chunk_at((y + NY - i) % NY), s_y.at[i], r_y.at[i], partner)
        for i in range(1, NY)
    ]
    x_copies = [
        remote(quarter(x), quarter(x), s_x.at[i], r_x.at[i], on_x(i)) for i in range(1, NX)
    ]
    x_arrivals = [
        remote(quarter((x + NX - i) % NX), quarter((x + NX - i) % NX), s_x.at[i], r_x.at[i], partner)
        for i in range(1, NX)
    ]

    def sink_exchange():
        @pl.when(gets_quarter)
        def _():
            spread(1).wait_recv()
            for c in a_copies:
                c.start()

    def sink_sum():
        @pl.when(x == 0)
        def _():
            for c in kept_copies:
                c.wait_recv()
            for j, u in enumerate(KEPT):
                chunk = ptab[u % 2, row_of(u, y), :].astype(F32)
                for i in range(1, NY):
                    chunk = chunk + scat[j, i].astype(F32)
                z_send[j] = chunk.astype(BF)
            kept_z.start()

        @pl.when(gets_quarter)
        def _():
            for c in a_copies:
                c.wait_recv()
            chunk = quart[part_of(y), :].astype(F32)
            for i in range(1, NY):
                chunk = chunk + scat[0, i].astype(F32)
            z_send[0] = chunk.astype(BF)
            z_copy.start()

    def sink_finish():
        @pl.when(x == 0)
        def _():
            kept_z.wait_recv()
            for j in range(1, len(KEPT)):
                c_send[j] = (z_send[j].astype(F32) + z_recv[j].astype(F32)).astype(BF)
                c_copies[j - 1].start()

        @pl.when(gets_quarter)
        def _():
            z_copy.wait_recv()

        @pl.when(gets_chunk)
        def _():
            c_arrival.wait_recv()

        @pl.when((x == 0) | gets_quarter)
        def _():
            chunk = z_send[0].astype(F32) + z_recv[0].astype(F32)
            tab[kvi, pl.ds(pl.multiple_of(base + y * CH, CH), CH), :] = chunk.astype(BF)

        for c in y_copies:
            c.start()

    def sink_along_x():
        for c in y_arrivals:
            c.wait_recv()
        for c in x_copies:
            c.start()

    attend(0, 0, [shard_block(2, 0, None)])
    send_kv(1)
    attend(0, 1, [shard_block(2, 1, None)])
    attend(0, 2, [shard_block(2, 2, None)])
    sink_exchange()
    hop(0)
    send_kv(2)
    bias_copy.wait_recv()
    near_blocks(0)
    sink_sum()
    hop(1)
    near_blocks(1)
    sink_finish()
    hop(2)
    far_blocks(0)
    near_blocks(2)
    sink_along_x()
    far_blocks(1)
    far_blocks(2)
    for c in x_arrivals:
        c.wait_recv()
    for h in range(HG):
        attend(0, h, [sink_block(h)])

    r_big = iota((ROWS, ROWS), 0)
    c_big = iota((ROWS, ROWS), 1)
    eye_big = (r_big == c_big).astype(BF)
    for h in range(HG):
        o_copies[h].wait_recv()
        ml_copies[h].wait_recv()
        m_a = ml[0, h, 0:1, :]
        m_b = ml_recv[h, 0:1, :]
        m_all = jnp.maximum(m_a, m_b)
        scale_a = jnp.exp(m_a - m_all)
        scale_b = jnp.exp(m_b - m_all)
        total = ml[0, h, 1:2, :] * scale_a + ml_recv[h, 1:2, :] * scale_b
        result = acc[0, h] * scale_a + o_recv[h].astype(F32) * scale_b
        result = (result / total).astype(BF)
        out_ref[:, h * HD:(h + 1) * HD] = lax.dot_general(
            eye_big, result, NT, preferred_element_type=F32
        ).astype(BF)

    @pl.when(x == 0)
    def _():
        for i in spread_to:
            spread(i).wait_send()

    for group in (q_copies, up, down, up2, down2, o_copies, ml_copies, y_copies, x_copies):
        for c in group:
            c.wait_send()
    bias_copy.wait_send()

    @pl.when(x == 0)
    def _():
        kept_z.wait_send()
        for c in kept_copies + c_copies:
            c.wait_send()

    @pl.when(gets_quarter)
    def _():
        z_copy.wait_send()
        for c in a_copies:
            c.wait_send()


def on_device(queries, keys, values, positions, tile_masks, sink_index):
    anywhere = pl.BlockSpec(memory_space=pl.ANY)
    dma = pltpu.SemaphoreType.DMA
    shard = (ROWS, HG * HD)
    return pl.pallas_call(
        kernel,
        out_shape=jax.ShapeDtypeStruct(shard, BF),
        in_specs=[anywhere] * 6,
        out_specs=pl.BlockSpec(memory_space=pltpu.VMEM),
        scratch_shapes=[
            pltpu.VMEM(shard, BF),
            pltpu.VMEM(shard, BF),
            pltpu.VMEM(shard, BF),
            pltpu.VMEM((3, ROWS), jnp.int32),
            pltpu.VMEM((1, SINK), jnp.int32),
            pltpu.SMEM((2, 2, 8), jnp.int32),
            pltpu.VMEM((5, HG, 2 * ROWS, HD), BF),
            pltpu.VMEM((2, HG, ROWS, HD), BF),
            pltpu.VMEM((8, ROWS), F32),
            pltpu.VMEM((8, ROWS), F32),
            pltpu.VMEM((8, ROWS), F32),
            pltpu.VMEM((2, HG, HD, ROWS), F32),
            pltpu.VMEM((2, HG, 8, ROWS), F32),
            pltpu.VMEM((HG, HD, ROWS), BF),
            pltpu.VMEM((HG, HD, ROWS), BF),
            pltpu.VMEM((HG, 8, ROWS), F32),
            pltpu.VMEM((2, SINK, HG * HD), BF),
            pltpu.VMEM((2, SINK, HG * HD), BF),
            pltpu.VMEM((SINK // 2, HG * HD), BF),
            pltpu.VMEM((len(KEPT), NY, CH, HG * HD), BF),
            pltpu.VMEM((len(KEPT), CH, HG * HD), BF),
            pltpu.VMEM((len(KEPT), CH, HG * HD), BF),
            pltpu.VMEM((len(KEPT), CH, HG * HD), BF),
            dma((6,)),
            dma((4, HG)), dma((4, HG)), dma((HG,)), dma((HG,)), dma, dma,
            dma((NX,)), dma, dma((len(KEPT), NY)), dma((len(KEPT), NY)), dma, dma,
            dma((len(KEPT),)), dma, dma((NY,)), dma((NY,)),
            dma((NX,)), dma((NX,)), dma((HG,)), dma((HG,)), dma((HG,)), dma((HG,)),
        ],
        compiler_params=pltpu.CompilerParams(
            collective_id=0, has_side_effects=True, vmem_limit_bytes=60 << 20
        ),
        cost_estimate=pl.CostEstimate(
            flops=2 * 10 * 2 * ROWS * ROWS * HD * HG, bytes_accessed=4 << 20,
            transcendentals=10 * ROWS * ROWS * HG,
        ),
    )(queries, keys, values, positions, sink_index[None, :], tile_masks.transpose(0, 2, 1))


def solution(mesh):
    in_specs = (
        P("tm", "heads"), P("tm", "heads"), P("tm", "heads"), P(None, "tm"), P("tm", None, None), P(),
    )
    return jax.shard_map(
        on_device, mesh=mesh, in_specs=in_specs, out_specs=P("tm", "heads"), check_vma=False
    )
```

```python
import functools

import jax
import jax.numpy as jnp
from jax import lax
from jax.experimental import pallas as pl
from jax.experimental.pallas import tpu as pltpu
from jax.sharding import PartitionSpec as P

MESH = pl.DeviceIdType.MESH
HG = 3
HD = 128
ROWS = 256
TILE = 128
SINK = 256
NX, NY = 4, 8
NP = NX * NY
CH = 16
KEPT = (0, 2)
MASKED = -1e30
FLOOR = -1e28
BF = jnp.bfloat16
F32 = jnp.float32
NT = (((1,), (1,)), ((), ()))


def iota(shape, dim):
    return lax.broadcasted_iota(jnp.int32, shape, dim)


def kernel(
    q_hbm, k_hbm, v_hbm, pos_hbm, sink_hbm, mask_hbm, out_ref,
    q_ref, k_ref, v_ref, pos_ref, sink_ref, mask_ref,
    kv, qb, bias_own, bias_send, bias_recv, acc, ml, o_send, o_recv, ml_recv,
    ptab, tab, quart, scat, z_send, z_recv, c_send,
    s_in, s_kv, r_kv, s_q, r_q, s_b, r_b, s_sc, r_sc, s_a, r_a, s_z, r_z, s_c, r_c, s_y, r_y,
    s_x, r_x, s_o, r_o, s_ml, r_ml,
):
    head = lax.axis_index("heads")
    me = lax.axis_index("tm")
    z = me % 2
    p = me // 2
    x = p // NY
    y = p % NY
    kvi = x % 2
    half = x // 2

    def dev(pp, zz):
        return (head, pp * 2 + zz)

    def remote(src, dst, ssem, rsem, target):
        return pltpu.make_async_remote_copy(
            src_ref=src, dst_ref=dst, send_sem=ssem, recv_sem=rsem,
            device_id=target, device_id_type=MESH,
        )

    partner = dev(p, 1 - z)
    after = dev((p + 1) % NP, z)
    before = dev((p + NP - 1) % NP, z)

    def on_y(i):
        return dev(x * NY + (y + i) % NY, z)

    def on_x(i):
        return dev(((x + i) % NX) * NY + y, z)

    near = [partner, after, before]
    near += [on_x(i) for i in range(1, NX)] + [on_y(i) for i in range(1, NY)]
    barrier = pltpu.get_barrier_semaphore()
    for target in near:
        pl.semaphore_signal(barrier, inc=1, device_id=target, device_id_type=MESH)

    loads = [
        pltpu.make_async_copy(src, dst, s_in.at[i])
        for i, (src, dst) in enumerate(
            [(pos_hbm, pos_ref), (k_hbm, k_ref), (v_hbm, v_ref), (sink_hbm, sink_ref),
             (mask_hbm, mask_ref), (q_hbm, q_ref)]
        )
    ]
    for c in loads:
        c.start()
    loads[0].wait()

    d_of = iota((HD, ROWS), 0)
    first = d_of < 16
    second = d_of < 72
    posf = pos_ref[...].astype(F32)
    coord = jnp.where(first, posf[0:1], jnp.where(second, posf[1:2], posf[2:3]))
    pair = jnp.where(first, d_of, jnp.where(second, d_of - 16, d_of - 72)) // 2
    width = jnp.where(first, 16.0, 56.0).astype(F32)
    inverse = jnp.exp2(pair.astype(F32) * (-16.0) / width)
    angle = (coord * inverse).T
    lane = iota((ROWS, HD), 1)
    cosine = jnp.cos(angle)
    sine = jnp.sin(angle)
    sine = jnp.where(lane % 2 == 0, -sine, sine)
    r_id = iota((HD, HD), 0)
    c_id = iota((HD, HD), 1)
    swap = (r_id + 1 - 2 * (r_id % 2) == c_id).astype(BF)
    eye = (r_id == c_id).astype(BF)

    def rotated(ref, h, factor):
        part = ref[:, h * HD:(h + 1) * HD]
        other = jnp.dot(part, swap, preferred_element_type=F32)
        return ((part.astype(F32) * cosine + other * sine) * factor).astype(BF)

    loads[1].wait()
    loads[2].wait()
    for h in range(HG):
        kv[2, h, 0:ROWS, :] = rotated(k_ref, h, 1.0)
        turned = lax.dot_general(
            eye, v_ref[:, h * HD:(h + 1) * HD], NT, preferred_element_type=F32
        ).astype(BF)
        kv[2, h, ROWS:ROWS + HD, :] = turned[:, 0:TILE]
        kv[2, h, ROWS + HD:ROWS + 2 * HD, :] = turned[:, TILE:]

    loads[3].wait()

    spread_to = [i for i in range(1, NX) if i not in KEPT]
    gets_quarter = functools.reduce(lambda a, b: a | b, [x == i for i in spread_to], x < 0)
    gets_chunk = functools.reduce(lambda a, b: a | b, [x == i for i in KEPT[1:]], x < 0)

    def spread(i):
        return remote(
            ptab.at[i % 2, pl.ds((i // 2) * (SINK // 2), SINK // 2)], quart,
            s_sc.at[i], r_sc, on_x(i),
        )

    @pl.when(x == 0)
    def _():
        sink_col = jnp.broadcast_to(sink_ref[...].astype(F32), (HD, SINK)).T.astype(jnp.int32)
        local = sink_col - me * ROWS
        hot = jnp.concatenate([local == lane, local == lane + HD], axis=1).astype(F32).astype(BF)
        for h in range(HG):
            cols = slice(h * HD, (h + 1) * HD)
            ptab[0, :, cols] = jnp.dot(
                hot, kv[2, h, 0:ROWS, :], preferred_element_type=F32
            ).astype(BF)
            ptab[1, :, cols] = jnp.dot(
                hot, v_ref[:, cols], preferred_element_type=F32
            ).astype(BF)

    pl.semaphore_wait(barrier, len(near))

    up = [remote(kv.at[2, h], kv.at[1, h], s_kv.at[0, h], r_kv.at[0, h], after) for h in range(HG)]
    down = [
        remote(kv.at[2, h], kv.at[3, h], s_kv.at[1, h], r_kv.at[1, h], before) for h in range(HG)
    ]
    up2 = [remote(kv.at[1, h], kv.at[0, h], s_kv.at[2, h], r_kv.at[2, h], after) for h in range(HG)]
    down2 = [
        remote(kv.at[3, h], kv.at[4, h], s_kv.at[3, h], r_kv.at[3, h], before) for h in range(HG)
    ]

    @pl.when(x == 0)
    def _():
        for i in spread_to:
            spread(i).start()

    def send_kv(h):
        @pl.when(p < NP - 1)
        def _():
            up[h].start()

        @pl.when(p > 0)
        def _():
            down[h].start()

    for slot, absent in ((0, p < 2), (1, p < 1), (3, p > NP - 2), (4, p > NP - 3)):
        @pl.when(absent)
        def _(slot=slot):
            kv[slot] = jnp.zeros((HG, 2 * ROWS, HD), BF)

    def row_of(u, yy):
        return pl.ds(pl.multiple_of((u // 2) * (SINK // 2) + yy * CH, CH), CH)

    kept_copies = [
        remote(
            ptab.at[u % 2, row_of(u, (y + i) % NY)], scat.at[j, i], s_a.at[j, i], r_a.at[j, i], on_y(i)
        )
        for j, u in enumerate(KEPT) for i in range(1, NY)
    ]

    @pl.when(x == 0)
    def _():
        for c in kept_copies:
            c.start()

    send_kv(0)


    loads[4].wait()
    loads[5].wait()
    for h in range(HG):
        qb[0, h] = rotated(q_ref, h, HD ** -0.5)
    wide = iota((1, ROWS), 1) < TILE

    def mask_row(offset, kt):
        slot = offset - 1 if offset > 0 else 4 - offset - 1
        other = me + offset
        inside = jnp.where((other >= 0) & (other < 2 * NP), 1, 0)
        both = [
            ((mask_ref[qt, kt, slot] * inside).astype(F32) - 1.0) * (-MASKED) for qt in range(2)
        ]
        return jnp.where(wide, both[0], both[1])

    for i, offset in enumerate((-3, -1, 1, 3)):
        for kt in range(2):
            bias_send[2 * i + kt:2 * i + kt + 1, :] = mask_row(offset, kt)
    bias_copy = remote(bias_send, bias_recv, s_b, r_b, partner)
    bias_copy.start()
    q_copies = [remote(qb.at[0, h], qb.at[1, h], s_q.at[h], r_q.at[h], partner) for h in range(HG)]
    for h in range(HG):
        q_copies[h].start()
    for i, offset in enumerate((-4, -2, 2, 4)):
        for kt in range(2):
            bias_own[2 * i + kt:2 * i + kt + 1, :] = mask_row(offset, kt)


    for t in range(2):
        for h in range(HG):
            ml[t, h, 0:1, :] = jnp.full((1, ROWS), FLOOR, F32)
            ml[t, h, 1:2, :] = jnp.zeros((1, ROWS), F32)
            acc[t, h] = jnp.zeros((HD, ROWS), F32)

    def attend(t, h, blocks):
        query = qb[t, h]
        m_old = ml[t, h, 0:1, :]
        m_new = m_old
        scores = []
        for key, _, rows in blocks:
            s = lax.dot_general(key(), query, NT, preferred_element_type=F32)
            for kt in range(2):
                part = jnp.max(s[kt * TILE:(kt + 1) * TILE], axis=0, keepdims=True)
                m_new = jnp.maximum(m_new, part if rows is None else part + rows[kt])
            scores.append(s)
        alpha = jnp.exp(m_old - m_new)
        total = ml[t, h, 1:2, :] * alpha
        result = acc[t, h] * alpha
        for (_, value, rows), s in zip(blocks, scores):
            weights = []
            for kt in range(2):
                level = m_new if rows is None else m_new - rows[kt]
                w = jnp.exp(s[kt * TILE:(kt + 1) * TILE] - level)
                total = total + jnp.sum(w, axis=0, keepdims=True)
                weights.append(w.astype(BF))
            result = result + jnp.dot(
                value(), jnp.concatenate(weights, axis=0), preferred_element_type=F32
            )
        acc[t, h] = result
        ml[t, h, 0:1, :] = m_new
        ml[t, h, 1:2, :] = total

    def shard_block(slot, h, rows):
        def key():
            return kv[slot, h, 0:ROWS, :]

        def value():
            return jnp.concatenate(
                [kv[slot, h, ROWS:ROWS + HD, :], kv[slot, h, ROWS + HD:ROWS + 2 * HD, :]], axis=1
            )

        return (key, value, rows)

    def own_rows(i):
        return [bias_own[2 * i + kt:2 * i + kt + 1, :] for kt in range(2)]

    def their_rows(even, odd):
        return [
            jnp.where(
                z == 0,
                bias_recv[2 * even + kt:2 * even + kt + 1, :],
                bias_recv[2 * odd + kt:2 * odd + kt + 1, :],
            )
            for kt in range(2)
        ]

    def sink_block(h):
        cols = slice(h * HD, (h + 1) * HD)

        def value():
            return lax.dot_general(eye, tab[1, :, cols], NT, preferred_element_type=F32).astype(BF)

        return (lambda: tab[0, :, cols], value, None)

    def hop(h):
        @pl.when(p > 0)
        def _():
            up[h].wait_recv()

        @pl.when((p > 0) & (p < NP - 1))
        def _():
            up2[h].start()

        @pl.when(p < NP - 1)
        def _():
            down[h].wait_recv()

        @pl.when((p > 0) & (p < NP - 1))
        def _():
            down2[h].start()

    def near_blocks(h):
        q_copies[h].wait_recv()
        attend(
            1,
            h,
            [
                shard_block(1, h, their_rows(0, 1)),
                shard_block(2, h, their_rows(1, 2)),
                shard_block(3, h, their_rows(2, 3)),
            ],
        )
        attend(0, h, [shard_block(1, h, own_rows(1)), shard_block(3, h, own_rows(2))])

    far = 4 * (1 - z)
    o_copies = [remote(o_send.at[h], o_recv.at[h], s_o.at[h], r_o.at[h], partner) for h in range(HG)]
    ml_copies = [
        remote(ml.at[1, h], ml_recv.at[h], s_ml.at[h], r_ml.at[h], partner) for h in range(HG)
    ]

    def far_blocks(h):
        @pl.when(p > 1)
        def _():
            up2[h].wait_recv()

        @pl.when(p < NP - 2)
        def _():
            down2[h].wait_recv()

        attend(1, h, [shard_block(far, h, their_rows(3, 0))])
        o_send[h] = acc[1, h].astype(BF)
        o_copies[h].start()
        ml_copies[h].start()
        attend(0, h, [shard_block(0, h, own_rows(0)), shard_block(4, h, own_rows(3))])

    base = half * (SINK // 2)

    def chunk_at(yy):
        return tab.at[kvi, pl.ds(pl.multiple_of(base + yy * CH, CH), CH)]

    def quarter(xx):
        row = pl.multiple_of((xx // 2) * (SINK // 2), SINK // 2)
        return tab.at[xx % 2, pl.ds(row, SINK // 2)]

    def part_of(yy):
        return pl.ds(pl.multiple_of(yy * CH, CH), CH)

    a_copies = [
        remote(quart.at[part_of((y + i) % NY)], scat.at[0, i], s_a.at[0, i], r_a.at[0, i], on_y(i))
        for i in range(1, NY)
    ]
    kept_z = remote(z_send, z_recv, s_z, r_z, partner)
    z_copy = remote(z_send.at[0], z_recv.at[0], s_z, r_z, partner)
    c_copies = [
        remote(c_send.at[j], tab.at[u % 2, row_of(u, y)], s_c.at[j], r_c, on_x(u))
        for j, u in enumerate(KEPT) if j > 0
    ]
    c_arrival = remote(c_send.at[0], chunk_at(y), s_c.at[0], r_c, partner)
    y_copies = [
        remote(chunk_at(y), chunk_at(y), s_y.at[i], r_y.at[i], on_y(i)) for i in range(1, NY)
    ]
    y_arrivals = [
        remote(chunk_at((y + NY - i) % NY), chunk_at((y + NY - i) % NY), s_y.at[i], r_y.at[i], partner)
        for i in range(1, NY)
    ]
    x_copies = [
        remote(quarter(x), quarter(x), s_x.at[i], r_x.at[i], on_x(i)) for i in range(1, NX)
    ]
    x_arrivals = [
        remote(quarter((x + NX - i) % NX), quarter((x + NX - i) % NX), s_x.at[i], r_x.at[i], partner)
        for i in range(1, NX)
    ]

    def sink_exchange():
        @pl.when(gets_quarter)
        def _():
            spread(1).wait_recv()
            for c in a_copies:
                c.start()

    def sink_sum():
        @pl.when(x == 0)
        def _():
            for c in kept_copies:
                c.wait_recv()
            for j, u in enumerate(KEPT):
                chunk = ptab[u % 2, row_of(u, y), :].astype(F32)
                for i in range(1, NY):
                    chunk = chunk + scat[j, i].astype(F32)
                z_send[j] = chunk.astype(BF)
            kept_z.start()

        @pl.when(gets_quarter)
        def _():
            for c in a_copies:
                c.wait_recv()
            chunk = quart[part_of(y), :].astype(F32)
            for i in range(1, NY):
                chunk = chunk + scat[0, i].astype(F32)
            z_send[0] = chunk.astype(BF)
            z_copy.start()

    def sink_finish():
        @pl.when(x == 0)
        def _():
            kept_z.wait_recv()
            for j in range(1, len(KEPT)):
                c_send[j] = (z_send[j].astype(F32) + z_recv[j].astype(F32)).astype(BF)
                c_copies[j - 1].start()

        @pl.when(gets_quarter)
        def _():
            z_copy.wait_recv()

        @pl.when(gets_chunk)
        def _():
            c_arrival.wait_recv()

        @pl.when((x == 0) | gets_quarter)
        def _():
            chunk = z_send[0].astype(F32) + z_recv[0].astype(F32)
            tab[kvi, pl.ds(pl.multiple_of(base + y * CH, CH), CH), :] = chunk.astype(BF)

        for c in y_copies:
            c.start()

    def sink_along_x():
        for c in y_arrivals:
            c.wait_recv()
        for c in x_copies:
            c.start()

    attend(0, 0, [shard_block(2, 0, None)])
    send_kv(1)
    attend(0, 1, [shard_block(2, 1, None)])
    attend(0, 2, [shard_block(2, 2, None)])
    sink_exchange()
    hop(0)
    send_kv(2)
    bias_copy.wait_recv()
    near_blocks(0)
    sink_sum()
    hop(1)
    near_blocks(1)
    sink_finish()
    hop(2)
    far_blocks(0)
    near_blocks(2)
    sink_along_x()
    far_blocks(1)
    far_blocks(2)
    for c in x_arrivals:
        c.wait_recv()
    for h in range(HG):
        attend(0, h, [sink_block(h)])

    r_big = iota((ROWS, ROWS), 0)
    c_big = iota((ROWS, ROWS), 1)
    eye_big = (r_big == c_big).astype(BF)
    for h in range(HG):
        o_copies[h].wait_recv()
        ml_copies[h].wait_recv()
        m_a = ml[0, h, 0:1, :]
        m_b = ml_recv[h, 0:1, :]
        m_all = jnp.maximum(m_a, m_b)
        scale_a = jnp.exp(m_a - m_all)
        scale_b = jnp.exp(m_b - m_all)
        total = ml[0, h, 1:2, :] * scale_a + ml_recv[h, 1:2, :] * scale_b
        result = acc[0, h] * scale_a + o_recv[h].astype(F32) * scale_b
        result = (result / total).astype(BF)
        out_ref[:, h * HD:(h + 1) * HD] = lax.dot_general(
            eye_big, result, NT, preferred_element_type=F32
        ).astype(BF)

    @pl.when(x == 0)
    def _():
        for i in spread_to:
            spread(i).wait_send()

    for h in range(HG):
        @pl.when(p < NP - 1)
        def _(h=h):
            up[h].wait_send()

        @pl.when(p > 0)
        def _(h=h):
            down[h].wait_send()

        @pl.when((p > 0) & (p < NP - 1))
        def _(h=h):
            up2[h].wait_send()
            down2[h].wait_send()

    for group in (q_copies, o_copies, ml_copies, y_copies, x_copies):
        for c in group:
            c.wait_send()
    bias_copy.wait_send()

    @pl.when(x == 0)
    def _():
        kept_z.wait_send()
        for c in kept_copies + c_copies:
            c.wait_send()

    @pl.when(gets_quarter)
    def _():
        z_copy.wait_send()
        for c in a_copies:
            c.wait_send()


def on_device(queries, keys, values, positions, tile_masks, sink_index):
    anywhere = pl.BlockSpec(memory_space=pl.ANY)
    dma = pltpu.SemaphoreType.DMA
    shard = (ROWS, HG * HD)
    return pl.pallas_call(
        kernel,
        out_shape=jax.ShapeDtypeStruct(shard, BF),
        in_specs=[anywhere] * 6,
        out_specs=pl.BlockSpec(memory_space=pltpu.VMEM),
        scratch_shapes=[
            pltpu.VMEM(shard, BF),
            pltpu.VMEM(shard, BF),
            pltpu.VMEM(shard, BF),
            pltpu.VMEM((3, ROWS), jnp.int32),
            pltpu.VMEM((1, SINK), jnp.int32),
            pltpu.SMEM((2, 2, 8), jnp.int32),
            pltpu.VMEM((5, HG, 2 * ROWS, HD), BF),
            pltpu.VMEM((2, HG, ROWS, HD), BF),
            pltpu.VMEM((8, ROWS), F32),
            pltpu.VMEM((8, ROWS), F32),
            pltpu.VMEM((8, ROWS), F32),
            pltpu.VMEM((2, HG, HD, ROWS), F32),
            pltpu.VMEM((2, HG, 8, ROWS), F32),
            pltpu.VMEM((HG, HD, ROWS), BF),
            pltpu.VMEM((HG, HD, ROWS), BF),
            pltpu.VMEM((HG, 8, ROWS), F32),
            pltpu.VMEM((2, SINK, HG * HD), BF),
            pltpu.VMEM((2, SINK, HG * HD), BF),
            pltpu.VMEM((SINK // 2, HG * HD), BF),
            pltpu.VMEM((len(KEPT), NY, CH, HG * HD), BF),
            pltpu.VMEM((len(KEPT), CH, HG * HD), BF),
            pltpu.VMEM((len(KEPT), CH, HG * HD), BF),
            pltpu.VMEM((len(KEPT), CH, HG * HD), BF),
            dma((6,)),
            dma((4, HG)), dma((4, HG)), dma((HG,)), dma((HG,)), dma, dma,
            dma((NX,)), dma, dma((len(KEPT), NY)), dma((len(KEPT), NY)), dma, dma,
            dma((len(KEPT),)), dma, dma((NY,)), dma((NY,)),
            dma((NX,)), dma((NX,)), dma((HG,)), dma((HG,)), dma((HG,)), dma((HG,)),
        ],
        compiler_params=pltpu.CompilerParams(
            collective_id=0, has_side_effects=True, vmem_limit_bytes=55000 << 10
        ),
        cost_estimate=pl.CostEstimate(
            flops=2 * 10 * 2 * ROWS * ROWS * HD * HG, bytes_accessed=4 << 20,
            transcendentals=10 * ROWS * ROWS * HG,
        ),
    )(queries, keys, values, positions, sink_index[None, :], tile_masks.transpose(0, 2, 1))


def solution(mesh):
    in_specs = (
        P("tm", "heads"), P("tm", "heads"), P("tm", "heads"), P(None, "tm"), P("tm", None, None), P(),
    )
    return jax.shard_map(
        on_device, mesh=mesh, in_specs=in_specs, out_specs=P("tm", "heads"), check_vma=False
    )
```

```python
import functools

import jax
import jax.numpy as jnp
from jax import lax
from jax.experimental import pallas as pl
from jax.experimental.pallas import tpu as pltpu
from jax.sharding import PartitionSpec as P

MESH = pl.DeviceIdType.MESH
HG = 3
HD = 128
ROWS = 256
TILE = 128
SINK = 256
NX, NY = 4, 8
NP = NX * NY
CH = 16
KEPT = (0, 2)
MASKED = -1e30
FLOOR = -1e28
BF = jnp.bfloat16
F32 = jnp.float32
NT = (((1,), (1,)), ((), ()))


def iota(shape, dim):
    return lax.broadcasted_iota(jnp.int32, shape, dim)


def kernel(
    q_hbm, k_hbm, v_hbm, pos_hbm, sink_hbm, mask_hbm, out_ref,
    q_ref, k_ref, v_ref, pos_ref, sink_ref, mask_ref,
    kv, qb, bias_own, bias_send, bias_recv, acc, ml, o_send, o_recv, ml_recv,
    ptab, tab, quart, scat, z_send, z_recv, c_send,
    s_in, s_kv, r_kv, s_q, r_q, s_b, r_b, s_sc, r_sc, s_a, r_a, s_z, r_z, s_c, r_c, s_y, r_y,
    s_x, r_x, s_o, r_o, s_ml, r_ml,
):
    head = lax.axis_index("heads")
    me = lax.axis_index("tm")
    z = me % 2
    p = me // 2
    x = p // NY
    y = p % NY
    kvi = x % 2
    half = x // 2

    def dev(pp, zz):
        return (head, pp * 2 + zz)

    def remote(src, dst, ssem, rsem, target):
        return pltpu.make_async_remote_copy(
            src_ref=src, dst_ref=dst, send_sem=ssem, recv_sem=rsem,
            device_id=target, device_id_type=MESH,
        )

    partner = dev(p, 1 - z)
    after = dev((p + 1) % NP, z)
    before = dev((p + NP - 1) % NP, z)

    def on_y(i):
        return dev(x * NY + (y + i) % NY, z)

    def on_x(i):
        return dev(((x + i) % NX) * NY + y, z)

    near = [partner, after, before]
    near += [on_x(i) for i in range(1, NX)] + [on_y(i) for i in range(1, NY)]
    barrier = pltpu.get_barrier_semaphore()
    for target in near:
        pl.semaphore_signal(barrier, inc=1, device_id=target, device_id_type=MESH)

    loads = [
        pltpu.make_async_copy(src, dst, s_in.at[i])
        for i, (src, dst) in enumerate(
            [(pos_hbm, pos_ref), (k_hbm, k_ref), (v_hbm, v_ref), (sink_hbm, sink_ref),
             (mask_hbm, mask_ref), (q_hbm, q_ref)]
        )
    ]
    for c in loads:
        c.start()
    loads[0].wait()

    d_of = iota((HD, ROWS), 0)
    first = d_of < 16
    second = d_of < 72
    posf = pos_ref[...].astype(F32)
    coord = jnp.where(first, posf[0:1], jnp.where(second, posf[1:2], posf[2:3]))
    pair = jnp.where(first, d_of, jnp.where(second, d_of - 16, d_of - 72)) // 2
    width = jnp.where(first, 16.0, 56.0).astype(F32)
    inverse = jnp.exp2(pair.astype(F32) * (-16.0) / width)
    angle = (coord * inverse).T
    lane = iota((ROWS, HD), 1)
    cosine = jnp.cos(angle)
    sine = jnp.sin(angle)
    sine = jnp.where(lane % 2 == 0, -sine, sine)
    r_id = iota((HD, HD), 0)
    c_id = iota((HD, HD), 1)
    swap = (r_id + 1 - 2 * (r_id % 2) == c_id).astype(BF)
    eye = (r_id == c_id).astype(BF)

    def rotated(ref, h, factor):
        part = ref[:, h * HD:(h + 1) * HD]
        other = jnp.dot(part, swap, preferred_element_type=F32)
        return ((part.astype(F32) * cosine + other * sine) * factor).astype(BF)

    loads[1].wait()
    loads[2].wait()
    for h in range(HG):
        kv[2, h, 0:ROWS, :] = rotated(k_ref, h, 1.0)
        turned = lax.dot_general(
            eye, v_ref[:, h * HD:(h + 1) * HD], NT, preferred_element_type=F32
        ).astype(BF)
        kv[2, h, ROWS:ROWS + HD, :] = turned[:, 0:TILE]
        kv[2, h, ROWS + HD:ROWS + 2 * HD, :] = turned[:, TILE:]

    loads[3].wait()

    spread_to = [i for i in range(1, NX) if i not in KEPT]
    gets_quarter = functools.reduce(lambda a, b: a | b, [x == i for i in spread_to], x < 0)
    gets_chunk = functools.reduce(lambda a, b: a | b, [x == i for i in KEPT[1:]], x < 0)

    def spread(i):
        return remote(
            ptab.at[i % 2, pl.ds((i // 2) * (SINK // 2), SINK // 2)], quart,
            s_sc.at[i], r_sc, on_x(i),
        )

    @pl.when(x == 0)
    def _():
        sink_col = jnp.broadcast_to(sink_ref[...].astype(F32), (HD, SINK)).T.astype(jnp.int32)
        local = sink_col - me * ROWS
        hot = jnp.concatenate([local == lane, local == lane + HD], axis=1).astype(F32).astype(BF)
        for h in range(HG):
            cols = slice(h * HD, (h + 1) * HD)
            ptab[0, :, cols] = jnp.dot(
                hot, kv[2, h, 0:ROWS, :], preferred_element_type=F32
            ).astype(BF)
            ptab[1, :, cols] = jnp.dot(
                hot, v_ref[:, cols], preferred_element_type=F32
            ).astype(BF)

    pl.semaphore_wait(barrier, len(near))

    up = [remote(kv.at[2, h], kv.at[1, h], s_kv.at[0, h], r_kv.at[0, h], after) for h in range(HG)]
    down = [
        remote(kv.at[2, h], kv.at[3, h], s_kv.at[1, h], r_kv.at[1, h], before) for h in range(HG)
    ]
    up2 = [remote(kv.at[1, h], kv.at[0, h], s_kv.at[2, h], r_kv.at[2, h], after) for h in range(HG)]
    down2 = [
        remote(kv.at[3, h], kv.at[4, h], s_kv.at[3, h], r_kv.at[3, h], before) for h in range(HG)
    ]

    @pl.when(x == 0)
    def _():
        for i in spread_to:
            spread(i).start()

    def send_kv(h):
        @pl.when(p < NP - 1)
        def _():
            up[h].start()

        @pl.when(p > 0)
        def _():
            down[h].start()

    for slot, absent in ((0, p < 2), (1, p < 1), (3, p > NP - 2), (4, p > NP - 3)):
        @pl.when(absent)
        def _(slot=slot):
            kv[slot] = jnp.zeros((HG, 2 * ROWS, HD), BF)

    def row_of(u, yy):
        return pl.ds(pl.multiple_of((u // 2) * (SINK // 2) + yy * CH, CH), CH)

    kept_copies = [
        remote(
            ptab.at[u % 2, row_of(u, (y + i) % NY)], scat.at[j, i], s_a.at[j, i], r_a.at[j, i], on_y(i)
        )
        for j, u in enumerate(KEPT) for i in range(1, NY)
    ]

    @pl.when(x == 0)
    def _():
        for c in kept_copies:
            c.start()

    send_kv(0)


    loads[4].wait()
    loads[5].wait()
    for h in range(HG):
        qb[0, h] = rotated(q_ref, h, HD ** -0.5)
    wide = iota((1, ROWS), 1) < TILE

    def mask_row(offset, kt):
        slot = offset - 1 if offset > 0 else 4 - offset - 1
        other = me + offset
        inside = jnp.where((other >= 0) & (other < 2 * NP), 1, 0)
        both = [
            ((mask_ref[qt, kt, slot] * inside).astype(F32) - 1.0) * (-MASKED) for qt in range(2)
        ]
        return jnp.where(wide, both[0], both[1])

    for i, offset in enumerate((-3, -1, 1, 3)):
        for kt in range(2):
            bias_send[2 * i + kt:2 * i + kt + 1, :] = mask_row(offset, kt)
    bias_copy = remote(bias_send, bias_recv, s_b, r_b, partner)
    bias_copy.start()
    q_copies = [remote(qb.at[0, h], qb.at[1, h], s_q.at[h], r_q.at[h], partner) for h in range(HG)]
    for h in range(HG):
        q_copies[h].start()
    for i, offset in enumerate((-4, -2, 2, 4)):
        for kt in range(2):
            bias_own[2 * i + kt:2 * i + kt + 1, :] = mask_row(offset, kt)


    for t in range(2):
        for h in range(HG):
            ml[t, h, 0:1, :] = jnp.full((1, ROWS), FLOOR, F32)
            ml[t, h, 1:2, :] = jnp.zeros((1, ROWS), F32)
            acc[t, h] = jnp.zeros((HD, ROWS), F32)

    def attend(t, h, blocks):
        query = qb[t, h]
        m_old = ml[t, h, 0:1, :]
        m_new = m_old
        scores = []
        for key, _, rows in blocks:
            s = lax.dot_general(key(), query, NT, preferred_element_type=F32)
            for kt in range(2):
                part = jnp.max(s[kt * TILE:(kt + 1) * TILE], axis=0, keepdims=True)
                m_new = jnp.maximum(m_new, part if rows is None else part + rows[kt])
            scores.append(s)
        alpha = jnp.exp(m_old - m_new)
        total = ml[t, h, 1:2, :] * alpha
        result = acc[t, h] * alpha
        for (_, value, rows), s in zip(blocks, scores):
            weights = []
            for kt in range(2):
                level = m_new if rows is None else m_new - rows[kt]
                w = jnp.exp(s[kt * TILE:(kt + 1) * TILE] - level)
                total = total + jnp.sum(w, axis=0, keepdims=True)
                weights.append(w.astype(BF))
            result = result + jnp.dot(
                value(), jnp.concatenate(weights, axis=0), preferred_element_type=F32
            )
        acc[t, h] = result
        ml[t, h, 0:1, :] = m_new
        ml[t, h, 1:2, :] = total

    def shard_block(slot, h, rows):
        def key():
            return kv[slot, h, 0:ROWS, :]

        def value():
            return jnp.concatenate(
                [kv[slot, h, ROWS:ROWS + HD, :], kv[slot, h, ROWS + HD:ROWS + 2 * HD, :]], axis=1
            )

        return (key, value, rows)

    def own_rows(i):
        return [bias_own[2 * i + kt:2 * i + kt + 1, :] for kt in range(2)]

    def their_rows(even, odd):
        return [
            jnp.where(
                z == 0,
                bias_recv[2 * even + kt:2 * even + kt + 1, :],
                bias_recv[2 * odd + kt:2 * odd + kt + 1, :],
            )
            for kt in range(2)
        ]

    def sink_block(h):
        cols = slice(h * HD, (h + 1) * HD)

        def value():
            return lax.dot_general(eye, tab[1, :, cols], NT, preferred_element_type=F32).astype(BF)

        return (lambda: tab[0, :, cols], value, None)

    def hop(h):
        @pl.when(p > 0)
        def _():
            up[h].wait_recv()

        @pl.when((p > 0) & (p < NP - 1))
        def _():
            up2[h].start()

        @pl.when(p < NP - 1)
        def _():
            down[h].wait_recv()

        @pl.when((p > 0) & (p < NP - 1))
        def _():
            down2[h].start()

    def near_blocks(h):
        q_copies[h].wait_recv()
        attend(
            1,
            h,
            [
                shard_block(1, h, their_rows(0, 1)),
                shard_block(2, h, their_rows(1, 2)),
                shard_block(3, h, their_rows(2, 3)),
            ],
        )
        attend(0, h, [shard_block(1, h, own_rows(1)), shard_block(3, h, own_rows(2))])

    far = 4 * (1 - z)
    o_copies = [remote(o_send.at[h], o_recv.at[h], s_o.at[h], r_o.at[h], partner) for h in range(HG)]
    ml_copies = [
        remote(ml.at[1, h], ml_recv.at[h], s_ml.at[h], r_ml.at[h], partner) for h in range(HG)
    ]

    def far_blocks(h):
        @pl.when(p > 1)
        def _():
            up2[h].wait_recv()

        @pl.when(p < NP - 2)
        def _():
            down2[h].wait_recv()

        attend(1, h, [shard_block(far, h, their_rows(3, 0))])
        o_send[h] = acc[1, h].astype(BF)
        o_copies[h].start()
        ml_copies[h].start()
        attend(0, h, [shard_block(0, h, own_rows(0)), shard_block(4, h, own_rows(3))])

    base = half * (SINK // 2)

    def chunk_at(yy):
        return tab.at[kvi, pl.ds(pl.multiple_of(base + yy * CH, CH), CH)]

    def quarter(xx):
        row = pl.multiple_of((xx // 2) * (SINK // 2), SINK // 2)
        return tab.at[xx % 2, pl.ds(row, SINK // 2)]

    def part_of(yy):
        return pl.ds(pl.multiple_of(yy * CH, CH), CH)

    a_copies = [
        remote(quart.at[part_of((y + i) % NY)], scat.at[0, i], s_a.at[0, i], r_a.at[0, i], on_y(i))
        for i in range(1, NY)
    ]
    kept_z = remote(z_send, z_recv, s_z, r_z, partner)
    z_copy = remote(z_send.at[0], z_recv.at[0], s_z, r_z, partner)
    c_copies = [
        remote(c_send.at[j], tab.at[u % 2, row_of(u, y)], s_c.at[j], r_c, on_x(u))
        for j, u in enumerate(KEPT) if j > 0
    ]
    c_arrival = remote(c_send.at[0], chunk_at(y), s_c.at[0], r_c, partner)
    y_copies = [
        remote(chunk_at(y), chunk_at(y), s_y.at[i], r_y.at[i], on_y(i)) for i in range(1, NY)
    ]
    y_arrivals = [
        remote(chunk_at((y + NY - i) % NY), chunk_at((y + NY - i) % NY), s_y.at[i], r_y.at[i], partner)
        for i in range(1, NY)
    ]
    x_copies = [
        remote(quarter(x), quarter(x), s_x.at[i], r_x.at[i], on_x(i)) for i in range(1, NX)
    ]
    x_arrivals = [
        remote(quarter((x + NX - i) % NX), quarter((x + NX - i) % NX), s_x.at[i], r_x.at[i], partner)
        for i in range(1, NX)
    ]

    def sink_exchange():
        @pl.when(gets_quarter)
        def _():
            spread(1).wait_recv()
            for c in a_copies:
                c.start()

    def sink_sum():
        @pl.when(x == 0)
        def _():
            for c in kept_copies:
                c.wait_recv()
            for j, u in enumerate(KEPT):
                chunk = ptab[u % 2, row_of(u, y), :].astype(F32)
                for i in range(1, NY):
                    chunk = chunk + scat[j, i].astype(F32)
                z_send[j] = chunk.astype(BF)
            kept_z.start()

        @pl.when(gets_quarter)
        def _():
            for c in a_copies:
                c.wait_recv()
            chunk = quart[part_of(y), :].astype(F32)
            for i in range(1, NY):
                chunk = chunk + scat[0, i].astype(F32)
            z_send[0] = chunk.astype(BF)
            z_copy.start()

    def sink_finish():
        @pl.when(x == 0)
        def _():
            kept_z.wait_recv()
            for j in range(1, len(KEPT)):
                c_send[j] = (z_send[j].astype(F32) + z_recv[j].astype(F32)).astype(BF)
                c_copies[j - 1].start()

        @pl.when(gets_quarter)
        def _():
            z_copy.wait_recv()

        @pl.when(gets_chunk)
        def _():
            c_arrival.wait_recv()

        @pl.when((x == 0) | gets_quarter)
        def _():
            chunk = z_send[0].astype(F32) + z_recv[0].astype(F32)
            tab[kvi, pl.ds(pl.multiple_of(base + y * CH, CH), CH), :] = chunk.astype(BF)

        for c in y_copies:
            c.start()

    def sink_along_x():
        for c in y_arrivals:
            c.wait_recv()
        for c in x_copies:
            c.start()

    attend(0, 0, [shard_block(2, 0, None)])
    send_kv(1)
    sink_exchange()
    attend(0, 1, [shard_block(2, 1, None)])
    attend(0, 2, [shard_block(2, 2, None)])
    hop(0)
    send_kv(2)
    bias_copy.wait_recv()
    near_blocks(0)
    sink_sum()
    hop(1)
    near_blocks(1)
    sink_finish()
    hop(2)
    far_blocks(0)
    near_blocks(2)
    sink_along_x()
    far_blocks(1)
    far_blocks(2)
    for c in x_arrivals:
        c.wait_recv()
    for h in range(HG):
        attend(0, h, [sink_block(h)])

    r_big = iota((ROWS, ROWS), 0)
    c_big = iota((ROWS, ROWS), 1)
    eye_big = (r_big == c_big).astype(BF)
    for h in range(HG):
        o_copies[h].wait_recv()
        ml_copies[h].wait_recv()
        m_a = ml[0, h, 0:1, :]
        m_b = ml_recv[h, 0:1, :]
        m_all = jnp.maximum(m_a, m_b)
        scale_a = jnp.exp(m_a - m_all)
        scale_b = jnp.exp(m_b - m_all)
        total = ml[0, h, 1:2, :] * scale_a + ml_recv[h, 1:2, :] * scale_b
        result = acc[0, h] * scale_a + o_recv[h].astype(F32) * scale_b
        result = (result / total).astype(BF)
        out_ref[:, h * HD:(h + 1) * HD] = lax.dot_general(
            eye_big, result, NT, preferred_element_type=F32
        ).astype(BF)

    @pl.when(x == 0)
    def _():
        for i in spread_to:
            spread(i).wait_send()

    for h in range(HG):
        @pl.when(p < NP - 1)
        def _(h=h):
            up[h].wait_send()

        @pl.when(p > 0)
        def _(h=h):
            down[h].wait_send()

        @pl.when((p > 0) & (p < NP - 1))
        def _(h=h):
            up2[h].wait_send()
            down2[h].wait_send()

    for group in (q_copies, o_copies, ml_copies, y_copies, x_copies):
        for c in group:
            c.wait_send()
    bias_copy.wait_send()

    @pl.when(x == 0)
    def _():
        kept_z.wait_send()
        for c in kept_copies + c_copies:
            c.wait_send()

    @pl.when(gets_quarter)
    def _():
        z_copy.wait_send()
        for c in a_copies:
            c.wait_send()


def on_device(queries, keys, values, positions, tile_masks, sink_index):
    anywhere = pl.BlockSpec(memory_space=pl.ANY)
    dma = pltpu.SemaphoreType.DMA
    shard = (ROWS, HG * HD)
    return pl.pallas_call(
        kernel,
        out_shape=jax.ShapeDtypeStruct(shard, BF),
        in_specs=[anywhere] * 6,
        out_specs=pl.BlockSpec(memory_space=pltpu.VMEM),
        scratch_shapes=[
            pltpu.VMEM(shard, BF),
            pltpu.VMEM(shard, BF),
            pltpu.VMEM(shard, BF),
            pltpu.VMEM((3, ROWS), jnp.int32),
            pltpu.VMEM((1, SINK), jnp.int32),
            pltpu.SMEM((2, 2, 8), jnp.int32),
            pltpu.VMEM((5, HG, 2 * ROWS, HD), BF),
            pltpu.VMEM((2, HG, ROWS, HD), BF),
            pltpu.VMEM((8, ROWS), F32),
            pltpu.VMEM((8, ROWS), F32),
            pltpu.VMEM((8, ROWS), F32),
            pltpu.VMEM((2, HG, HD, ROWS), F32),
            pltpu.VMEM((2, HG, 8, ROWS), F32),
            pltpu.VMEM((HG, HD, ROWS), BF),
            pltpu.VMEM((HG, HD, ROWS), BF),
            pltpu.VMEM((HG, 8, ROWS), F32),
            pltpu.VMEM((2, SINK, HG * HD), BF),
            pltpu.VMEM((2, SINK, HG * HD), BF),
            pltpu.VMEM((SINK // 2, HG * HD), BF),
            pltpu.VMEM((len(KEPT), NY, CH, HG * HD), BF),
            pltpu.VMEM((len(KEPT), CH, HG * HD), BF),
            pltpu.VMEM((len(KEPT), CH, HG * HD), BF),
            pltpu.VMEM((len(KEPT), CH, HG * HD), BF),
            dma((6,)),
            dma((4, HG)), dma((4, HG)), dma((HG,)), dma((HG,)), dma, dma,
            dma((NX,)), dma, dma((len(KEPT), NY)), dma((len(KEPT), NY)), dma, dma,
            dma((len(KEPT),)), dma, dma((NY,)), dma((NY,)),
            dma((NX,)), dma((NX,)), dma((HG,)), dma((HG,)), dma((HG,)), dma((HG,)),
        ],
        compiler_params=pltpu.CompilerParams(
            collective_id=0, has_side_effects=True, vmem_limit_bytes=55000 << 10
        ),
        cost_estimate=pl.CostEstimate(
            flops=2 * 10 * 2 * ROWS * ROWS * HD * HG, bytes_accessed=4 << 20,
            transcendentals=10 * ROWS * ROWS * HG,
        ),
    )(queries, keys, values, positions, sink_index[None, :], tile_masks.transpose(0, 2, 1))


def solution(mesh):
    in_specs = (
        P("tm", "heads"), P("tm", "heads"), P("tm", "heads"), P(None, "tm"), P("tm", None, None), P(),
    )
    return jax.shard_map(
        on_device, mesh=mesh, in_specs=in_specs, out_specs=P("tm", "heads"), check_vma=False
    )
```
